768 devices in a mesh: row: 32 (over y, x), col: 24 (over z, core).
Axes of the slice: x: 4, y: 8, z: 12, core: 2. Of those that a mesh axis runs over, the one named last changes fastest.
Arguments:
- x_stack: float32 [32, 24, 4, 128, 128], P('row', 'col'), may hold values from -6 to 6
- s_stack: float32 [32, 24, 4, 128, 128], P('row', 'col'), may hold values from -0.5 to 0.5
- entries: int32 [32, 24, 2, 4], P('row', 'col'), may hold values from 0 to 7, as said below
- counts: int32 [32, 24], P('row', 'col'), may hold values from 2 to 4, as said below
Outputs:
- y_stack: float32 [32, 24, 4, 128, 128], P('row', 'col')
The draws below stay inside these ranges and needn't reach their ends.
Inputs may be any that keep to these rules, and one draw needn't show every extreme that they name: `entries`: in every device's stack all 4 slots name distinct blocks of its 6 x 8 region; entry 0 is below 6, entry 1 below 8. `counts`: some device's stack is full.
All inputs are finite; a program needn't handle non-finite values.
Results may differ from the reference program's by a relative error of at most 0.0003.
Values sent between devices are 32-bit elements; how exact they have to be, the bound alone decides.
No kernel may reach another device: no remote copies, remote signals or barrier semaphores. Data moves between devices by JAX's collectives and lax.ppermute only.
A program may use at most 128 MiB of HBM per device.

```python
import jax
import jax.numpy as jnp
from jax import lax

BS = 128
CAP = 4
RB = 6
CB = 8
N_ROW = 32
N_COL = 24


def draw_entries(key, part):
    key = jax.random.fold_in(key, 11)
    region = RB * CB
    scores = jax.random.randint(key, (N_ROW, N_COL, region), 0, 65536)
    scores = scores * region + jnp.arange(region, dtype=jnp.int32)
    picked = jnp.argsort(scores, axis=-1)[:, :, :CAP].astype(jnp.int32)
    local_rows = picked // CB
    local_cols = picked % CB
    return jnp.stack([local_rows, local_cols], axis=2).astype(jnp.int32)


def draw_counts(key, part):
    key = jax.random.fold_in(key, 12)
    first_key, second_key = jax.random.split(key)
    base = jax.random.randint(first_key, (N_ROW * N_COL,), CAP // 2, CAP + 1)
    chosen = jax.random.randint(second_key, (), 0, N_ROW * N_COL)
    base = base.at[chosen].set(CAP)
    return base.reshape(N_ROW, N_COL).astype(jnp.int32)


def block_scale(stream_key, extent, shards, smallest, top_value):
    factor_of, own = 1.0, jax.random.fold_in(stream_key, 6)
    for dim, shards_of in shards:
        draws = jnp.exp(jax.random.uniform(jax.random.fold_in(own, dim), (shards_of,), jnp.float32, smallest / len(shards), top_value / len(shards)))
        factor_of = factor_of * jnp.repeat(draws, extent[dim] // shards_of).reshape([-1 if axis == dim else 1 for axis in range(len(extent))])
    return factor_of


def noise(own_key, dims, width, reach, shards=(), kind=jnp.bfloat16):
    loudness = block_scale(own_key, dims, shards, -0.22, 0.18) if shards else 1.0
    values = jax.random.normal(own_key, dims, jnp.float32) * width * loudness
    return jnp.minimum(jnp.maximum(values, -reach), reach).astype(kind)


def setup_inputs(seed: int = 0) -> dict:
    seeds = jax.random.split(jax.random.key(seed), 5)
    x_stack = noise(seeds[0], (N_ROW, N_COL, CAP, BS, BS), 1.0, 6.0, ((0, 32), (1, 24)), jnp.float32)
    s_stack = noise(seeds[1], (N_ROW, N_COL, CAP, BS, BS), BS ** -0.5, 0.5, ((0, 32), (1, 24)), jnp.float32)
    entries = draw_entries(jax.random.fold_in(seeds[4], 71), 0)
    counts = draw_counts(jax.random.fold_in(seeds[4], 71), 0)
    return dict(x_stack=x_stack, s_stack=s_stack, entries=entries, counts=counts)


def accumulate(running, x_row, e_row, c_row, s_col, e_col, c_col, own_rows, own_cols):
    capacity = x_row.shape[2]
    tile_size = x_row.shape[3]
    slot_ids = jnp.arange(capacity, dtype=jnp.int32)
    panel_width = x_row.shape[1]
    row_flat = x_row.reshape(panel_width * capacity, tile_size, tile_size)
    owners = jnp.arange(panel_width, dtype=jnp.int32)[:, None]
    left_rows = e_row[0, :, 0].reshape(-1)
    left_inner = (owners * CB + e_row[0, :, 1]).reshape(-1)
    left_valid = (slot_ids[None, :] < c_row[0][:, None]).reshape(-1)
    positions = jnp.arange(left_rows.shape[0], dtype=jnp.int32)
    piece_rows = s_col.shape[0]
    holders = jnp.arange(piece_rows, dtype=jnp.int32)[:, None]
    right_flat = s_col.reshape(piece_rows * capacity, tile_size, tile_size)
    right_inner = (holders * RB + e_col[:, 0, 0]).reshape(-1)
    right_cols = e_col[:, 0, 1].reshape(-1)
    right_valid = (slot_ids[None, :] < c_col[:, 0][:, None]).reshape(-1)
    matched = (own_rows[:, None, None] == left_rows[None, None, :]) & (own_cols[:, None, None] == right_cols[None, :, None]) & (right_inner[None, :, None] == left_inner[None, None, :]) & right_valid[None, :, None] & left_valid[None, None, :]
    chosen_at = jnp.sum(jnp.where(matched, positions, 0), axis=2).astype(jnp.int32)
    present = jnp.any(matched, axis=2)
    chosen = jnp.where(present[:, :, None, None], row_flat[chosen_at], 0.0)
    return running + jnp.einsum("ofab,fbc->oac", chosen, right_flat, precision=lax.Precision.HIGHEST)


def reference(x_stack, s_stack, entries, counts):
    capacity = x_stack.shape[2]
    tile_size = x_stack.shape[3]
    slot_ids = jnp.arange(capacity, dtype=jnp.int32)

    def one_device(flat_id):
        row_id = (flat_id // N_COL).astype(jnp.int32)
        col_id = (flat_id % N_COL).astype(jnp.int32)
        x_row = lax.dynamic_index_in_dim(x_stack, row_id, 0, keepdims=True)
        e_row = lax.dynamic_index_in_dim(entries, row_id, 0, keepdims=True)
        c_row = lax.dynamic_index_in_dim(counts, row_id, 0, keepdims=True)
        s_col = lax.dynamic_index_in_dim(s_stack, col_id, 1, keepdims=True)
        e_col = lax.dynamic_index_in_dim(entries, col_id, 1, keepdims=True)
        c_col = lax.dynamic_index_in_dim(counts, col_id, 1, keepdims=True)
        own_entries = lax.dynamic_index_in_dim(e_row[0], col_id, 0, keepdims=False)
        own_tiles = lax.dynamic_index_in_dim(x_row[0], col_id, 0, keepdims=False)
        own_count = lax.dynamic_index_in_dim(c_row[0], col_id, 0, keepdims=False)
        zeroed = jnp.zeros((capacity, tile_size, tile_size), jnp.float32)
        product = accumulate(zeroed, x_row, e_row, c_row, s_col, e_col, c_col, own_entries[0], own_entries[1])
        own_valid = slot_ids < own_count
        return jnp.where(own_valid[:, None, None], 1.5 * own_tiles - 0.5 * product, 0.0)

    result = lax.map(one_device, jnp.arange(N_ROW * N_COL, dtype=jnp.int32))
    return result.reshape(N_ROW, N_COL, capacity, tile_size, tile_size)
```

```python
import functools

import jax
import jax.numpy as jnp
from jax import lax
from jax.experimental import pallas as pl
from jax.experimental.pallas import tpu as pltpu
from jax.sharding import PartitionSpec as P

RB = 6
CB = 8
CAP = 4
BS = 128
ROUND = 12

HIGHEST = lax.Precision.HIGHEST
VMEM_LIMIT = 48 * 1024 * 1024


def dot_nt(a, b):
    return lax.dot_general(a, b, (((1,), (1,)), ((), ())), preferred_element_type=jnp.float32)


def pack_kernel(n_row, own_ref, slots_ref, s_ref, out_ref):
    n_col = slots_ref.shape[0]
    rows_out = out_ref.shape[0] // n_row
    piece = BS // n_row
    for e in range(CAP):
        for q in range(piece):
            out_ref[pl.ds(e * piece + q, n_row, stride=rows_out), :] = s_ref[e, q * n_row : (q + 1) * n_row, :]
    slots = slots_ref[...].astype(jnp.float32)
    lane_k = lax.broadcasted_iota(jnp.int32, (n_col, 2 * BS), 1)
    of_col = lax.broadcasted_iota(jnp.int32, (n_col, 2 * BS), 0)
    spread = jnp.where(lane_k // CB == of_col, 1.0, 0.0)
    fields = lax.dot_general(slots, spread, (((0,), (0,)), ((), ())), preferred_element_type=jnp.float32)[:16].astype(jnp.int32)
    k = lax.broadcasted_iota(jnp.int32, (1, 2 * BS), 1)
    within = lax.rem(k, CB)
    owner = lax.div(k, CB)
    held = fields[8:9]
    count = own_ref[8]
    head, tail = [], []
    for o in range(CAP):
        block_row, block_col = own_ref[o], own_ref[CAP + o]
        valid = (o < count).astype(jnp.int32)
        place = jnp.zeros((1, 2 * BS), jnp.int32)
        for e in range(CAP):
            hit = (fields[CAP + e : CAP + e + 1] == within) & (fields[e : e + 1] == block_row) & (e < held)
            place = jnp.where(hit, owner * CAP + e + 1, place)
        place = jnp.where(owner < n_col, place * valid, 0)
        place = jnp.where(k == 192, block_row, place)
        place = jnp.where(k == 193, block_col, place)
        place = jnp.where(k == 194, valid, place)
        head.append(place[:, :BS])
        tail.append(place[:, BS:])
    table = jnp.concatenate(head + tail, axis=0).astype(jnp.float32)
    for m in range(n_row):
        out_ref[m * rows_out + CAP * piece : (m + 1) * rows_out, :] = table


def select_kernel(n_row, where_ref, got_ref, out_ref, plan_ref, m_ref, sel_ref):
    rows_in = got_ref.shape[0] // n_row
    piece = BS // n_row
    base = CAP * piece
    slots = CAP * n_row
    me, first = where_ref[0], where_ref[1]

    def strided(start):
        return got_ref[pl.ds(start, n_row, stride=rows_in), :]

    head = jnp.concatenate([strided(base + o) for o in range(CAP)], axis=0)
    tail = jnp.concatenate([strided(base + CAP + o) for o in range(CAP)], axis=0)
    lane = lax.broadcasted_iota(jnp.int32, (slots, BS), 1)
    holder = lax.rem(lax.broadcasted_iota(jnp.int32, (slots, 1), 0), n_row)
    meta = tail[:, 64:67].astype(jnp.int32)
    inner = holder * RB + meta[:, 0:1]
    block_col = meta[:, 1:2]
    valid = meta[:, 2:3] > 0
    at_head = jnp.where((lane == inner) & valid, 1.0, 0.0)
    at_tail = jnp.where((lane + BS == inner) & valid, 1.0, 0.0)
    of_col = jnp.where(lane == block_col, 1.0, 0.0)
    m = (dot_nt(head, at_head) + dot_nt(tail, at_tail)) * dot_nt(of_col, of_col)
    m_ref[...] = m
    need = m[:n_row]
    for o in range(1, CAP):
        need = jnp.maximum(need, m[o * n_row : (o + 1) * n_row])
    need = jnp.where(need > 0.5, 1.0, 0.0)
    before = jnp.where(
        lax.broadcasted_iota(jnp.int32, (slots, slots), 0) < lax.broadcasted_iota(jnp.int32, (slots, slots), 1), 1.0, 0.0
    )
    rank = jnp.dot(need, before, preferred_element_type=jnp.float32).astype(jnp.int32) - first
    rank = jnp.where(need > 0.5, rank, -1)
    chosen = jnp.concatenate([jnp.where(rank == p, 1.0, 0.0) for p in range(ROUND)], axis=0)
    sel_ref[...] = chosen
    for q in range(piece):
        rows = jnp.concatenate([strided(e * piece + q) for e in range(CAP)], axis=0)
        part = jnp.dot(chosen, rows, precision=HIGHEST, preferred_element_type=jnp.float32)
        for p in range(ROUND):
            out_ref[pl.ds(p * piece + q, n_row, stride=ROUND * piece), :] = part[p * n_row : (p + 1) * n_row]
    row = lax.broadcasted_iota(jnp.int32, (n_row, BS), 0)
    mine = row == me
    own_m = [jnp.sum(jnp.where(mine, m[o * n_row : (o + 1) * n_row], 0.0), axis=0, keepdims=True) for o in range(CAP)]
    own_sel = [
        jnp.sum(jnp.where(mine, chosen[p * n_row : (p + 1) * n_row], 0.0), axis=0, keepdims=True) for p in range(ROUND)
    ]
    pad = [jnp.zeros((BS - ROUND, BS), jnp.float32)]
    plan = dot_nt(jnp.concatenate(own_m + [jnp.zeros((4, BS), jnp.float32)], axis=0), jnp.concatenate(own_sel + pad, axis=0))
    most = jnp.max(jnp.sum(need, axis=1, keepdims=True), axis=0, keepdims=True)
    plan = jnp.where(lax.broadcasted_iota(jnp.int32, (8, BS), 0) == 7, most, plan)
    plan_ref[...] = (plan + 0.5).astype(jnp.int32)


def multiply_kernel(n_row, plan_ref, base_ref, got_ref, x_ref, out_ref, x_buf, sems):
    piece = BS // n_row

    def tile_copy(o, p):
        return pltpu.make_async_copy(x_ref.at[plan_ref[o, p] - 1], x_buf.at[o, p], sems.at[o, p])

    for p in range(ROUND):
        for o in range(CAP):

            @pl.when(plan_ref[o, p] > 0)
            def _():
                tile_copy(o, p).start()

    out_ref[...] = base_ref[...]
    for p in range(ROUND):
        used = plan_ref[0, p]
        for o in range(1, CAP):
            used = used + plan_ref[o, p]

        @pl.when(used > 0)
        def _():
            s_tile = jnp.concatenate(
                [got_ref[pl.ds(p * piece + q, n_row, stride=ROUND * piece), :] for q in range(piece)], axis=0
            )
            for o in range(CAP):

                @pl.when(plan_ref[o, p] > 0)
                def _():
                    tile_copy(o, p).wait()
                    product = jnp.dot(x_buf[o, p], s_tile, precision=HIGHEST, preferred_element_type=jnp.float32)
                    out_ref[o] = out_ref[o] - 0.5 * product


def per_device(n_row, n_col, x_stack, s_stack, entries, counts):
    smem = pl.BlockSpec(memory_space=pltpu.SMEM)
    vmem = pl.BlockSpec(memory_space=pltpu.VMEM)
    params = pltpu.CompilerParams(vmem_limit_bytes=VMEM_LIMIT)
    piece = BS // n_row
    x_own = x_stack[0, 0]
    row_panel = lax.all_gather(x_stack[0], "col", axis=0, tiled=True).reshape(n_col * CAP, BS, BS)

    own = jnp.concatenate([entries.reshape(2 * CAP), counts.reshape(1), jnp.zeros((BS - 2 * CAP - 1,), jnp.int32)])
    slots = lax.all_to_all(jnp.broadcast_to(own[None, None], (n_col, 1, BS)), "col", 0, 0)

    rows_out = CAP * piece + 2 * CAP
    packed = pl.pallas_call(
        functools.partial(pack_kernel, n_row),
        out_shape=jax.ShapeDtypeStruct((n_row * rows_out, BS), jnp.float32),
        in_specs=[smem, vmem, vmem],
        out_specs=vmem,
        compiler_params=params,
        name="pack",
    )(own, slots.reshape(n_col, BS), s_stack[0, 0])
    pieces = lax.all_to_all(packed.reshape(n_row, rows_out, BS), "row", 0, 0).reshape(n_row * rows_out, BS)

    me = lax.axis_index("row").astype(jnp.int32)

    def one_round(first, base):
        chosen, plan = pl.pallas_call(
            functools.partial(select_kernel, n_row),
            out_shape=(
                jax.ShapeDtypeStruct((n_row * ROUND * piece, BS), jnp.float32),
                jax.ShapeDtypeStruct((8, BS), jnp.int32),
            ),
            in_specs=[smem, vmem],
            out_specs=(vmem, vmem),
            scratch_shapes=[pltpu.VMEM((CAP * n_row, BS), jnp.float32), pltpu.VMEM((ROUND * n_row, BS), jnp.float32)],
            compiler_params=params,
            name="select",
        )(jnp.stack([me, first]), pieces)
        tiles = lax.all_to_all(chosen.reshape(n_row, ROUND * piece, BS), "row", 0, 0)
        result = pl.pallas_call(
            functools.partial(multiply_kernel, n_row),
            out_shape=jax.ShapeDtypeStruct((CAP, BS, BS), jnp.float32),
            in_specs=[smem, vmem, vmem, pl.BlockSpec(memory_space=pl.ANY)],
            out_specs=vmem,
            scratch_shapes=[
                pltpu.VMEM((CAP, ROUND, BS, BS), jnp.float32),
                pltpu.SemaphoreType.DMA((CAP, ROUND)),
            ],
            compiler_params=params,
            name="multiply",
        )(plan, base, tiles.reshape(n_row * ROUND * piece, BS), row_panel)
        return plan, result

    valid = jnp.arange(CAP, dtype=jnp.int32) < counts[0, 0]
    base = jnp.where(valid[:, None, None], 1.5 * x_own, 0.0)
    plan, result = one_round(jnp.int32(0), base)
    most = plan[7, 0]

    def another(state):
        first, partial = state
        return first + ROUND, one_round(first, partial)[1]

    _, result = lax.while_loop(lambda state: state[0] < most, another, (jnp.int32(ROUND), result))
    return result[None, None]


def solution(mesh):
    return jax.shard_map(
        functools.partial(per_device, mesh.shape["row"], mesh.shape["col"]),
        mesh=mesh,
        in_specs=(
            P("row", "col", None, None, None),
            P("row", "col", None, None, None),
            P("row", "col", None, None),
            P("row", "col"),
        ),
        out_specs=P("row", "col", None, None, None),
        check_vma=False,
    )
```

```python
import functools

import jax
import jax.numpy as jnp
from jax import lax
from jax.experimental import pallas as pl
from jax.experimental.pallas import tpu as pltpu
from jax.sharding import PartitionSpec as P

RB = 6
CB = 8
CAP = 4
BS = 128
ROUND = 12
TABLE = 2

VMEM_LIMIT = 48 * 1024 * 1024


def iota(shape, dim):
    return lax.broadcasted_iota(jnp.int32, shape, dim)


def dot(a, b, dims=((1,), (0,))):
    return lax.dot_general(a, b, (dims, ((), ())), preferred_element_type=jnp.float32)


def split(a, parts):
    out = []
    for _ in range(parts):
        out.append(a.astype(jnp.bfloat16))
        a = a - out[-1].astype(jnp.float32)
    return out


def cut_kernel(n_row, s_ref, out_ref):
    piece = BS // n_row
    rows_out = CAP * piece + TABLE
    for e in range(CAP):
        for q in range(piece):
            out_ref[pl.ds(e * piece + q, n_row, stride=rows_out), :] = s_ref[e, q * n_row : (q + 1) * n_row, :]
    for t in range(TABLE):
        out_ref[pl.ds(CAP * piece + t, n_row, stride=rows_out), :] = jnp.zeros((n_row, BS), jnp.float32)


def pack_kernel(n_row, n_col, slots_ref, cut_ref, out_ref):
    piece = BS // n_row
    rows_out = CAP * piece + TABLE
    out_ref[...] = cut_ref[...]
    of_slot = lax.rem(iota((BS, BS), 1), CAP)
    field = iota((BS, BS), 0)
    mine = iota((n_col, BS), 0) == lax.div(iota((n_col, BS), 1), CAP)
    got = slots_ref[...].reshape(n_col, BS).astype(jnp.float32)

    def along(at):
        spread = jnp.where(field == at, 1.0, 0.0)
        return jnp.sum(jnp.where(mine, dot(got, spread), 0.0), axis=0, keepdims=True)

    used = lax.rem(iota((1, BS), 1), CAP).astype(jnp.float32) < along(2 * CAP)
    block_row = jnp.where(used, along(of_slot), -1.0)
    block_col = along(of_slot + CAP)
    out_ref[pl.ds(CAP * piece, n_row, stride=rows_out), :] = jnp.broadcast_to(block_row, (n_row, BS))
    out_ref[pl.ds(CAP * piece + 1, n_row, stride=rows_out), :] = jnp.broadcast_to(block_col, (n_row, BS))


def select_kernel(n_row, first_ref, got_ref, out_ref, plan_ref):
    piece = BS // n_row
    rows_in = CAP * piece + TABLE
    base = CAP * piece
    slots = CAP * n_row
    my_row, my_col, first = lax.axis_index("row"), lax.axis_index("col"), first_ref[0]

    def strided(start):
        return got_ref[pl.ds(start, n_row, stride=rows_in), :]

    block_row, block_col = strided(base), strided(base + 1)
    lane = iota((n_row, BS), 1)
    own_row, own_col = [], []
    for o in range(CAP):
        here = lane == my_col * CAP + o
        own_row.append(jnp.sum(jnp.where(here, block_row, 0.0), axis=1, keepdims=True))
        own_col.append(jnp.sum(jnp.where(here, block_col, 0.0), axis=1, keepdims=True))
    both = jnp.concatenate([block_row, block_col], axis=0)
    of_slot, of_k = iota((BS, 2 * BS), 0), iota((BS, 2 * BS), 1)
    k = iota((n_row, 2 * BS), 1)
    within = lax.rem(k, CB).astype(jnp.float32)
    place = (lax.div(k, CB) * CAP + 1).astype(jnp.float32)
    spread = [dot(both, jnp.where(of_slot == lax.div(of_k, CB) * CAP + e, 1.0, 0.0)) for e in range(CAP)]
    in_col = [spread[e][n_row:] == within for e in range(CAP)]
    tables = []
    for o in range(CAP):
        wanted = jnp.where(own_row[o] < 0.0, -2.0, own_row[o])
        found = jnp.zeros((n_row, 2 * BS), jnp.float32)
        for e in range(CAP):
            found = jnp.where(in_col[e] & (spread[e][:n_row] == wanted), place + e, found)
        tables.append(found)
    table = jnp.concatenate(tables, axis=0)
    holds_row = jnp.concatenate(own_row, axis=0).astype(jnp.int32)
    holds_col = jnp.concatenate(own_col, axis=0).astype(jnp.int32)
    inner = lax.rem(iota((slots, 1), 0), n_row) * RB + holds_row
    valid = holds_row >= 0
    wide = iota((slots, BS), 1)
    at_head = jnp.where((wide == inner) & valid, 1.0, 0.0)
    at_tail = jnp.where((wide + BS == inner) & valid, 1.0, 0.0)
    of_col = jnp.where(wide == holds_col, 1.0, 0.0)
    nt = ((1,), (1,))
    m = (dot(table[:, :BS], at_head, nt) + dot(table[:, BS:], at_tail, nt)) * dot(of_col, of_col, nt)
    need = m[:n_row]
    for o in range(1, CAP):
        need = jnp.maximum(need, m[o * n_row : (o + 1) * n_row])
    need = jnp.where(need > 0.5, 1.0, 0.0)
    before = jnp.where(iota((slots, slots), 0) < iota((slots, slots), 1), 1.0, 0.0)
    rank = dot(need, before).astype(jnp.int32) - first
    rank = jnp.where(need > 0.5, rank, -1)
    chosen = jnp.concatenate([jnp.where(rank == p, 1.0, 0.0) for p in range(ROUND)], axis=0)
    rows = jnp.concatenate(
        [jnp.concatenate([strided(e * piece + q) for e in range(CAP)], axis=0) for q in range(piece)], axis=1
    )
    pick = chosen.astype(jnp.bfloat16)
    high, mid, low = split(rows, 3)
    part = dot(pick, high) + dot(pick, mid) + dot(pick, low)
    for q in range(piece):
        for p in range(ROUND):
            out_ref[pl.ds(p * piece + q, n_row, stride=ROUND * piece), :] = part[
                p * n_row : (p + 1) * n_row, q * BS : (q + 1) * BS
            ]
    mine = iota((n_row, BS), 0) == my_row

    def own(a, n):
        return [jnp.sum(jnp.where(mine, a[i * n_row : (i + 1) * n_row], 0.0), axis=0, keepdims=True) for i in range(n)]

    own_m = jnp.concatenate(own(m, CAP) + [jnp.zeros((4, BS), jnp.float32)], axis=0)
    own_chosen = jnp.concatenate(own(chosen, ROUND) + [jnp.zeros((BS - ROUND, BS), jnp.float32)], axis=0)
    most = jnp.max(jnp.sum(need, axis=1, keepdims=True), axis=0, keepdims=True)
    plan = jnp.where(iota((8, BS), 0) == 7, most, dot(own_m, own_chosen, nt))
    plan_ref[...] = (plan + 0.5).astype(jnp.int32)


def multiply_kernel(n_row, plan_ref, base_ref, got_ref, x_ref, out_ref, x_buf, sems):
    piece = BS // n_row

    def tile_copy(o, p):
        return pltpu.make_async_copy(x_ref.at[plan_ref[o, p] - 1], x_buf.at[o, p], sems.at[o, p])

    for p in range(ROUND):
        for o in range(CAP):

            @pl.when(plan_ref[o, p] > 0)
            def _():
                tile_copy(o, p).start()

    out_ref[...] = base_ref[...]
    for p in range(ROUND):
        used = plan_ref[0, p]
        for o in range(1, CAP):
            used = used + plan_ref[o, p]

        @pl.when(used > 0)
        def _():
            s_tile = jnp.concatenate(
                [got_ref[pl.ds(p * piece + q, n_row, stride=ROUND * piece), :] for q in range(piece)], axis=0
            )
            s_high, s_low = split(s_tile, 2)
            for o in range(CAP):

                @pl.when(plan_ref[o, p] > 0)
                def _():
                    tile_copy(o, p).wait()
                    x_high, x_low = split(x_buf[o, p], 2)
                    product = dot(x_high, s_high) + (dot(x_high, s_low) + dot(x_low, s_high))
                    out_ref[o] = out_ref[o] - 0.5 * product


def per_device(n_row, n_col, x_stack, s_stack, entries, counts):
    smem = pl.BlockSpec(memory_space=pltpu.SMEM)
    vmem = pl.BlockSpec(memory_space=pltpu.VMEM)
    hbm = pl.BlockSpec(memory_space=pltpu.HBM)
    params = pltpu.CompilerParams(vmem_limit_bytes=VMEM_LIMIT)
    piece = BS // n_row
    rows_out = CAP * piece + TABLE
    x_own = x_stack[0, 0]
    row_panel = lax.all_gather(x_stack[0], "col", axis=0, tiled=True).reshape(n_col * CAP, BS, BS)

    own = jnp.concatenate([entries.reshape(2 * CAP), counts.reshape(1), jnp.zeros((BS - 2 * CAP - 1,), jnp.int32)])
    slots = lax.all_to_all(jnp.broadcast_to(own[None, None], (n_col, 1, BS)), "col", 0, 0)
    cut = pl.pallas_call(
        functools.partial(cut_kernel, n_row),
        out_shape=jax.ShapeDtypeStruct((n_row * rows_out, BS), jnp.float32),
        in_specs=[vmem],
        out_specs=vmem,
        compiler_params=params,
        cost_estimate=pl.CostEstimate(flops=0, bytes_accessed=2**22, transcendentals=0),
        name="cut",
    )(s_stack[0, 0])
    packed = pl.pallas_call(
        functools.partial(pack_kernel, n_row, n_col),
        out_shape=jax.ShapeDtypeStruct((n_row * rows_out, BS), jnp.float32),
        in_specs=[vmem, vmem],
        out_specs=vmem,
        compiler_params=params,
        name="pack",
    )(slots, cut)
    parts = rows_out // 2
    pieces = lax.all_to_all(packed.reshape(n_row, parts, 2, BS), "row", 0, 0).reshape(n_row * rows_out, BS)

    def one_round(first, base):
        chosen, plan = pl.pallas_call(
            functools.partial(select_kernel, n_row),
            out_shape=(
                jax.ShapeDtypeStruct((n_row * ROUND * piece, BS), jnp.float32),
                jax.ShapeDtypeStruct((8, BS), jnp.int32),
            ),
            in_specs=[smem, vmem],
            out_specs=(vmem, vmem),
            compiler_params=params,
            name="select",
        )(first.reshape(1), pieces)
        tiles = lax.all_to_all(chosen.reshape(n_row, ROUND * piece, BS), "row", 0, 0)
        result = pl.pallas_call(
            functools.partial(multiply_kernel, n_row),
            out_shape=jax.ShapeDtypeStruct((CAP, BS, BS), jnp.float32),
            in_specs=[smem, vmem, vmem, hbm],
            out_specs=vmem,
            scratch_shapes=[
                pltpu.VMEM((CAP, ROUND, BS, BS), jnp.float32),
                pltpu.SemaphoreType.DMA((CAP, ROUND)),
            ],
            compiler_params=params,
            name="multiply",
        )(plan, base, tiles.reshape(n_row * ROUND * piece, BS), row_panel)
        return plan, result

    valid = jnp.arange(CAP, dtype=jnp.int32) < counts[0, 0]
    base = jnp.where(valid[:, None, None], 1.5 * x_own, 0.0)
    plan, result = one_round(jnp.zeros((), jnp.int32), base)
    most = plan[7, 0]

    def another(state):
        first, partial = state
        return first + ROUND, one_round(first, partial)[1]

    _, result = lax.while_loop(lambda state: state[0] < most, another, (jnp.int32(ROUND), result))
    return result[None, None]


def solution(mesh):
    return jax.shard_map(
        functools.partial(per_device, mesh.shape["row"], mesh.shape["col"]),
        mesh=mesh,
        in_specs=(
            P("row", "col", None, None, None),
            P("row", "col", None, None, None),
            P("row", "col", None, None),
            P("row", "col"),
        ),
        out_specs=P("row", "col", None, None, None),
        check_vma=False,
    )
```

```python
import functools

import jax
import jax.numpy as jnp
from jax import lax
from jax.experimental import pallas as pl
from jax.experimental.pallas import tpu as pltpu
from jax.sharding import PartitionSpec as P

RB = 6
CB = 8
CAP = 4
BS = 128
ROUND = 12
AHEAD = 16
TABLE = 2

VMEM_LIMIT = 24 * 1024 * 1024


def iota(shape, dim):
    return lax.broadcasted_iota(jnp.int32, shape, dim)


def dot(a, b, dims=((1,), (0,))):
    return lax.dot_general(a, b, (dims, ((), ())), preferred_element_type=jnp.float32)


def split(a, parts):
    out = []
    for _ in range(parts):
        out.append(a.astype(jnp.bfloat16))
        a = a - out[-1].astype(jnp.float32)
    return out


def cut_kernel(n_row, s_ref, out_ref):
    piece = BS // n_row
    rows_out = CAP * piece + TABLE
    for e in range(CAP):
        for q in range(piece):
            out_ref[pl.ds(e * piece + q, n_row, stride=rows_out), :] = s_ref[e, q * n_row : (q + 1) * n_row, :]
    for t in range(TABLE):
        out_ref[pl.ds(CAP * piece + t, n_row, stride=rows_out), :] = jnp.zeros((n_row, BS), jnp.float32)


def pack_kernel(n_row, n_col, slots_ref, cut_ref, ahead_ref, out_ref):
    piece = BS // n_row
    rows_out = CAP * piece + TABLE
    out_ref[...] = cut_ref[...]
    of_slot = lax.rem(iota((BS, BS), 1), CAP)
    field = iota((BS, BS), 0)
    mine = iota((n_col, BS), 0) == lax.div(iota((n_col, BS), 1), CAP)
    got = slots_ref[...].reshape(n_col, BS).astype(jnp.float32)

    def along(at):
        spread = jnp.where(field == at, 1.0, 0.0)
        return jnp.sum(jnp.where(mine, dot(got, spread), 0.0), axis=0, keepdims=True)

    used = lax.rem(iota((1, BS), 1), CAP).astype(jnp.float32) < along(2 * CAP)
    block_row = jnp.where(used, along(of_slot), -1.0)
    block_col = along(of_slot + CAP)
    out_ref[pl.ds(CAP * piece, n_row, stride=rows_out), :] = jnp.broadcast_to(block_row, (n_row, BS))
    out_ref[pl.ds(CAP * piece + 1, n_row, stride=rows_out), :] = jnp.broadcast_to(block_col, (n_row, BS))


def select_kernel(n_row, first_ref, got_ref, out_ref, plan_ref, most_ref):
    piece = BS // n_row
    rows_in = CAP * piece + TABLE
    base = CAP * piece
    slots = CAP * n_row
    my_row, my_col, first = lax.axis_index("row"), lax.axis_index("col"), first_ref[0]

    def strided(start):
        return got_ref[pl.ds(start, n_row, stride=rows_in), :]

    block_row, block_col = strided(base), strided(base + 1)
    lane = iota((n_row, BS), 1)
    own_row, own_col = [], []
    for o in range(CAP):
        here = lane == my_col * CAP + o
        own_row.append(jnp.sum(jnp.where(here, block_row, 0.0), axis=1, keepdims=True))
        own_col.append(jnp.sum(jnp.where(here, block_col, 0.0), axis=1, keepdims=True))
    both = jnp.concatenate([block_row, block_col], axis=0)
    of_slot, of_k = iota((BS, 2 * BS), 0), iota((BS, 2 * BS), 1)
    k = iota((n_row, 2 * BS), 1)
    within = lax.rem(k, CB).astype(jnp.float32)
    place = (lax.div(k, CB) * CAP + 1).astype(jnp.float32)
    spread = [dot(both, jnp.where(of_slot == lax.div(of_k, CB) * CAP + e, 1.0, 0.0)) for e in range(CAP)]
    in_col = [spread[e][n_row:] == within for e in range(CAP)]
    tables = []
    for o in range(CAP):
        wanted = jnp.where(own_row[o] < 0.0, -2.0, own_row[o])
        found = jnp.zeros((n_row, 2 * BS), jnp.float32)
        for e in range(CAP):
            found = jnp.where(in_col[e] & (spread[e][:n_row] == wanted), place + e, found)
        tables.append(found)
    table = jnp.concatenate(tables, axis=0)
    holds_row = jnp.concatenate(own_row, axis=0).astype(jnp.int32)
    holds_col = jnp.concatenate(own_col, axis=0).astype(jnp.int32)
    inner = lax.rem(iota((slots, 1), 0), n_row) * RB + holds_row
    valid = holds_row >= 0
    wide = iota((slots, BS), 1)
    at_head = jnp.where((wide == inner) & valid, 1.0, 0.0)
    at_tail = jnp.where((wide + BS == inner) & valid, 1.0, 0.0)
    of_col = jnp.where(wide == holds_col, 1.0, 0.0)
    nt = ((1,), (1,))
    m = (dot(table[:, :BS], at_head, nt) + dot(table[:, BS:], at_tail, nt)) * dot(of_col, of_col, nt)
    need = m[:n_row]
    for o in range(1, CAP):
        need = jnp.maximum(need, m[o * n_row : (o + 1) * n_row])
    need = jnp.where(need > 0.5, 1.0, 0.0)
    before = jnp.where(iota((slots, slots), 0) < iota((slots, slots), 1), 1.0, 0.0)
    rank = dot(need, before).astype(jnp.int32) - first
    rank = jnp.where(need > 0.5, rank, -1)
    chosen = jnp.concatenate([jnp.where(rank == p, 1.0, 0.0) for p in range(ROUND)], axis=0)
    rows = jnp.concatenate(
        [jnp.concatenate([strided(e * piece + q) for e in range(CAP)], axis=0) for q in range(piece)], axis=1
    )
    pick = chosen.astype(jnp.bfloat16)
    high, mid, low = split(rows, 3)
    part = dot(pick, high) + dot(pick, mid) + dot(pick, low)
    for q in range(piece):
        for p in range(ROUND):
            out_ref[pl.ds(p * piece + q, n_row, stride=ROUND * piece), :] = part[
                p * n_row : (p + 1) * n_row, q * BS : (q + 1) * BS
            ]
    mine = iota((n_row, BS), 0) == my_row

    def own(a, n):
        return [jnp.sum(jnp.where(mine, a[i * n_row : (i + 1) * n_row], 0.0), axis=0, keepdims=True) for i in range(n)]

    own_m = jnp.concatenate(own(m, CAP) + [jnp.zeros((4, BS), jnp.float32)], axis=0)
    own_chosen = jnp.concatenate(own(chosen, ROUND) + [jnp.zeros((BS - ROUND, BS), jnp.float32)], axis=0)
    needed = jnp.sum(need, axis=1, keepdims=True)
    most_ref[0, 0] = (jnp.max(needed) + 0.5).astype(jnp.int32)
    here = jnp.sum(jnp.sum(own_chosen, axis=1, keepdims=True), axis=0, keepdims=True)
    plan = jnp.where(iota((8, BS), 0) == 7, here, dot(own_m, own_chosen, nt))
    plan_ref[...] = (plan + 0.5).astype(jnp.int32)


def each_product(plan_ref, act):
    def tile(p, n):
        for o in range(CAP):
            used = plan_ref[o, p] > 0

            @pl.when(used)
            def _():
                act(n, o, p)

            n = n + used.astype(jnp.int32)
        return n

    lax.fori_loop(0, plan_ref[7, 0], tile, 0)


def fetch_kernel(plan_ref, x_ref, out_ref, sems):
    def copy(n, o, p):
        return pltpu.make_async_copy(x_ref.at[plan_ref[o, p] - 1], out_ref.at[n], sems.at[n])

    def start(n, o, p):
        @pl.when(n < AHEAD)
        def _():
            copy(n, o, p).start()

    def wait(n, o, p):
        @pl.when(n < AHEAD)
        def _():
            copy(n, o, p).wait()

    each_product(plan_ref, start)
    each_product(plan_ref, wait)


def multiply_kernel(n_row, plan_ref, base_ref, got_ref, ahead_ref, x_ref, out_ref, x_buf, sem):
    piece = BS // n_row
    out_ref[...] = base_ref[...]

    def act(n, o, p):
        s_tile = jnp.concatenate(
            [got_ref[pl.ds(p * piece + q, n_row, stride=ROUND * piece), :] for q in range(piece)], axis=0
        )
        s_high, s_low = split(s_tile, 2)

        @pl.when(n < AHEAD)
        def _():
            x_buf[...] = ahead_ref[jnp.minimum(n, AHEAD - 1)]

        @pl.when(n >= AHEAD)
        def _():
            copy = pltpu.make_async_copy(x_ref.at[plan_ref[o, p] - 1], x_buf, sem)
            copy.start()
            copy.wait()

        x_high, x_low = split(x_buf[...], 2)
        product = dot(x_high, s_high) + (dot(x_high, s_low) + dot(x_low, s_high))
        out_ref[o] = out_ref[o] - 0.5 * product

    each_product(plan_ref, act)


def per_device(n_row, n_col, x_stack, s_stack, entries, counts):
    smem = pl.BlockSpec(memory_space=pltpu.SMEM)
    vmem = pl.BlockSpec(memory_space=pltpu.VMEM)
    hbm = pl.BlockSpec(memory_space=pltpu.HBM)
    params = pltpu.CompilerParams(vmem_limit_bytes=VMEM_LIMIT)
    piece = BS // n_row
    rows_out = CAP * piece + TABLE
    x_own = x_stack[0, 0]
    row_panel = lax.all_gather(x_stack[0], "col", axis=0, tiled=True).reshape(n_col * CAP, BS, BS)

    valid = jnp.arange(CAP, dtype=jnp.int32) < counts[0, 0]
    base = jnp.where(valid[:, None, None], 1.5 * x_own, 0.0)
    own = jnp.concatenate([entries.reshape(2 * CAP), counts.reshape(1), jnp.zeros((BS - 2 * CAP - 1,), jnp.int32)])
    slots = lax.all_to_all(jnp.broadcast_to(own[None, None], (n_col, 1, BS)), "col", 0, 0)
    cut = pl.pallas_call(
        functools.partial(cut_kernel, n_row),
        out_shape=jax.ShapeDtypeStruct((n_row * rows_out, BS), jnp.float32),
        in_specs=[vmem],
        out_specs=vmem,
        compiler_params=params,
        cost_estimate=pl.CostEstimate(flops=0, bytes_accessed=2**22, transcendentals=0),
        name="cut",
    )(s_stack[0, 0])
    packed = pl.pallas_call(
        functools.partial(pack_kernel, n_row, n_col),
        out_shape=jax.ShapeDtypeStruct((n_row * rows_out, BS), jnp.float32),
        in_specs=[vmem, vmem, pl.BlockSpec(memory_space=pl.ANY)],
        out_specs=vmem,
        compiler_params=params,
        name="pack",
    )(slots, cut, base)
    parts = rows_out // 2
    pieces = lax.all_to_all(packed.reshape(n_row, parts, 2, BS), "row", 0, 0).reshape(n_row * rows_out, BS)

    def select(first):
        chosen, plan, most = pl.pallas_call(
            functools.partial(select_kernel, n_row),
            out_shape=(
                jax.ShapeDtypeStruct((n_row * ROUND * piece, BS), jnp.float32),
                jax.ShapeDtypeStruct((8, BS), jnp.int32),
                jax.ShapeDtypeStruct((1, 1), jnp.int32),
            ),
            in_specs=[smem, vmem],
            out_specs=(vmem, vmem, smem),
            compiler_params=params,
            name="select",
        )(first.reshape(1), pieces)
        tiles = lax.all_to_all(chosen.reshape(n_row, ROUND * piece, BS), "row", 0, 0)
        return tiles.reshape(n_row * ROUND * piece, BS), plan, most[0, 0]

    def multiply(tiles, plan, base):
        x_tiles = pl.pallas_call(
            fetch_kernel,
            out_shape=jax.ShapeDtypeStruct((AHEAD, BS, BS), jnp.float32),
            in_specs=[smem, hbm],
            out_specs=vmem,
            scratch_shapes=[pltpu.SemaphoreType.DMA((AHEAD,))],
            compiler_params=params,
            cost_estimate=pl.CostEstimate(flops=0, bytes_accessed=2**23, transcendentals=0),
            name="fetch",
        )(plan, row_panel)
        return pl.pallas_call(
            functools.partial(multiply_kernel, n_row),
            out_shape=jax.ShapeDtypeStruct((CAP, BS, BS), jnp.float32),
            in_specs=[smem, vmem, vmem, vmem, hbm],
            out_specs=vmem,
            scratch_shapes=[pltpu.VMEM((BS, BS), jnp.float32), pltpu.SemaphoreType.DMA],
            compiler_params=params,
            name="multiply",
        )(plan, base, tiles, x_tiles, row_panel)

    tiles, plan, most = select(jnp.zeros((), jnp.int32))

    def another(state):
        first, partial = state
        more, where, _ = select(first)
        return first + ROUND, multiply(more, where, partial)

    result = multiply(tiles, plan, base)
    _, result = lax.while_loop(lambda state: state[0] < most, another, (jnp.int32(ROUND), result))
    return result[None, None]


def solution(mesh):
    return jax.shard_map(
        functools.partial(per_device, mesh.shape["row"], mesh.shape["col"]),
        mesh=mesh,
        in_specs=(
            P("row", "col", None, None, None),
            P("row", "col", None, None, None),
            P("row", "col", None, None),
            P("row", "col"),
        ),
        out_specs=P("row", "col", None, None, None),
        check_vma=False,
    )
```

```python
import functools

import jax
import jax.numpy as jnp
from jax import lax
from jax.experimental import pallas as pl
from jax.experimental.pallas import tpu as pltpu
from jax.sharding import PartitionSpec as P

RB = 6
CB = 8
CAP = 4
BS = 128
ROUND = 12
AHEAD = 16
TABLE = 2

VMEM_LIMIT = 24 * 1024 * 1024


def iota(shape, dim):
    return lax.broadcasted_iota(jnp.int32, shape, dim)


def dot(a, b, dims=((1,), (0,))):
    return lax.dot_general(a, b, (dims, ((), ())), preferred_element_type=jnp.float32)


def split(a, parts):
    out = []
    for _ in range(parts):
        out.append(a.astype(jnp.bfloat16))
        a = a - out[-1].astype(jnp.float32)
    return out


def cut_kernel(n_row, s_ref, out_ref):
    piece = BS // n_row
    rows_out = CAP * piece + TABLE
    for e in range(CAP):
        for q in range(piece):
            out_ref[pl.ds(e * piece + q, n_row, stride=rows_out), :] = s_ref[e, q * n_row : (q + 1) * n_row, :]
    for t in range(TABLE):
        out_ref[pl.ds(CAP * piece + t, n_row, stride=rows_out), :] = jnp.zeros((n_row, BS), jnp.float32)


def pack_kernel(n_row, n_col, slots_ref, cut_ref, ahead_ref, out_ref):
    piece = BS // n_row
    rows_out = CAP * piece + TABLE
    out_ref[...] = cut_ref[...]
    of_slot = lax.rem(iota((BS, BS), 1), CAP)
    field = iota((BS, BS), 0)
    mine = iota((n_col, BS), 0) == lax.div(iota((n_col, BS), 1), CAP)
    got = slots_ref[...].reshape(n_col, BS).astype(jnp.float32)

    def along(at):
        spread = jnp.where(field == at, 1.0, 0.0)
        return jnp.sum(jnp.where(mine, dot(got, spread), 0.0), axis=0, keepdims=True)

    used = lax.rem(iota((1, BS), 1), CAP).astype(jnp.float32) < along(2 * CAP)
    block_row = jnp.where(used, along(of_slot), -1.0)
    block_col = along(of_slot + CAP)
    out_ref[pl.ds(CAP * piece, n_row, stride=rows_out), :] = jnp.broadcast_to(block_row, (n_row, BS))
    out_ref[pl.ds(CAP * piece + 1, n_row, stride=rows_out), :] = jnp.broadcast_to(block_col, (n_row, BS))


def select_kernel(n_row, initial, *refs):
    got_ref, out_ref, plan_ref, most_ref = refs[-4:]
    piece = BS // n_row
    rows_in = CAP * piece + TABLE
    base = CAP * piece
    slots = CAP * n_row
    my_row, my_col, first = lax.axis_index("row"), lax.axis_index("col"), 0 if initial else refs[0][0]

    def strided(start):
        return got_ref[pl.ds(start, n_row, stride=rows_in), :]

    block_row, block_col = strided(base), strided(base + 1)
    lane = iota((n_row, BS), 1)
    own_row, own_col = [], []
    for o in range(CAP):
        here = lane == my_col * CAP + o
        own_row.append(jnp.sum(jnp.where(here, block_row, 0.0), axis=1, keepdims=True))
        own_col.append(jnp.sum(jnp.where(here, block_col, 0.0), axis=1, keepdims=True))
    both = jnp.concatenate([block_row, block_col], axis=0)
    of_slot, of_k = iota((BS, 2 * BS), 0), iota((BS, 2 * BS), 1)
    k = iota((n_row, 2 * BS), 1)
    within = lax.rem(k, CB).astype(jnp.float32)
    place = (lax.div(k, CB) * CAP + 1).astype(jnp.float32)
    spread = [dot(both, jnp.where(of_slot == lax.div(of_k, CB) * CAP + e, 1.0, 0.0)) for e in range(CAP)]
    in_col = [spread[e][n_row:] == within for e in range(CAP)]
    tables = []
    for o in range(CAP):
        wanted = jnp.where(own_row[o] < 0.0, -2.0, own_row[o])
        found = jnp.zeros((n_row, 2 * BS), jnp.float32)
        for e in range(CAP):
            found = jnp.where(in_col[e] & (spread[e][:n_row] == wanted), place + e, found)
        tables.append(found)
    table = jnp.concatenate(tables, axis=0)
    holds_row = jnp.concatenate(own_row, axis=0).astype(jnp.int32)
    holds_col = jnp.concatenate(own_col, axis=0).astype(jnp.int32)
    inner = lax.rem(iota((slots, 1), 0), n_row) * RB + holds_row
    valid = holds_row >= 0
    wide = iota((slots, BS), 1)
    at_head = jnp.where((wide == inner) & valid, 1.0, 0.0)
    at_tail = jnp.where((wide + BS == inner) & valid, 1.0, 0.0)
    of_col = jnp.where(wide == holds_col, 1.0, 0.0)
    nt = ((1,), (1,))
    m = (dot(table[:, :BS], at_head, nt) + dot(table[:, BS:], at_tail, nt)) * dot(of_col, of_col, nt)
    need = m[:n_row]
    for o in range(1, CAP):
        need = jnp.maximum(need, m[o * n_row : (o + 1) * n_row])
    need = jnp.where(need > 0.5, 1.0, 0.0)
    before = jnp.where(iota((slots, slots), 0) < iota((slots, slots), 1), 1.0, 0.0)
    rank = dot(need, before).astype(jnp.int32) - first
    rank = jnp.where(need > 0.5, rank, -1)
    chosen = jnp.concatenate([jnp.where(rank == p, 1.0, 0.0) for p in range(ROUND)], axis=0)
    rows = jnp.concatenate(
        [jnp.concatenate([strided(e * piece + q) for e in range(CAP)], axis=0) for q in range(piece)], axis=1
    )
    pick = jnp.concatenate([chosen.astype(jnp.bfloat16)] * 3, axis=1)
    part = dot(pick, jnp.concatenate(split(rows, 3), axis=0))
    for q in range(piece):
        for p in range(ROUND):
            out_ref[pl.ds(p * piece + q, n_row, stride=ROUND * piece), :] = part[
                p * n_row : (p + 1) * n_row, q * BS : (q + 1) * BS
            ]
    mine = iota((n_row, BS), 0) == my_row

    def own(a, n):
        return [jnp.sum(jnp.where(mine, a[i * n_row : (i + 1) * n_row], 0.0), axis=0, keepdims=True) for i in range(n)]

    own_m = jnp.concatenate(own(m, CAP) + [jnp.zeros((4, BS), jnp.float32)], axis=0)
    own_chosen = jnp.concatenate(own(chosen, ROUND) + [jnp.zeros((BS - ROUND, BS), jnp.float32)], axis=0)
    needed = jnp.sum(need, axis=1, keepdims=True)
    most_ref[0, 0] = (jnp.max(needed) + 0.5).astype(jnp.int32)
    here = jnp.sum(jnp.sum(own_chosen, axis=1, keepdims=True), axis=0, keepdims=True)
    plan = jnp.where(iota((8, BS), 0) == 7, here, dot(own_m, own_chosen, nt))
    plan_ref[...] = (plan + 0.5).astype(jnp.int32)


def each_product(plan_ref, act):
    def tile(p, n):
        for o in range(CAP):
            used = plan_ref[o, p] > 0

            @pl.when(used)
            def _():
                act(n, o, p)

            n = n + used.astype(jnp.int32)
        return n

    lax.fori_loop(0, plan_ref[7, 0], tile, 0)


def fetch_kernel(plan_ref, x_ref, out_ref, sems):
    def copy(n, o, p):
        return pltpu.make_async_copy(x_ref.at[plan_ref[o, p] - 1], out_ref.at[n], sems.at[n])

    def start(n, o, p):
        @pl.when(n < AHEAD)
        def _():
            copy(n, o, p).start()

    def wait(n, o, p):
        @pl.when(n < AHEAD)
        def _():
            copy(n, o, p).wait()

    each_product(plan_ref, start)
    each_product(plan_ref, wait)


def multiply_kernel(n_row, plan_ref, base_ref, got_ref, ahead_ref, x_ref, out_ref, x_buf, sem):
    piece = BS // n_row
    out_ref[...] = base_ref[...]

    def act(n, o, p):
        s_tile = jnp.concatenate(
            [got_ref[pl.ds(p * piece + q, n_row, stride=ROUND * piece), :] for q in range(piece)], axis=0
        )
        s_high, s_low = split(s_tile, 2)

        @pl.when(n < AHEAD)
        def _():
            x_buf[...] = ahead_ref[jnp.minimum(n, AHEAD - 1)]

        @pl.when(n >= AHEAD)
        def _():
            copy = pltpu.make_async_copy(x_ref.at[plan_ref[o, p] - 1], x_buf, sem)
            copy.start()
            copy.wait()

        x_high, x_low = split(x_buf[...], 2)
        product = dot(x_high, s_high) + (dot(x_high, s_low) + dot(x_low, s_high))
        out_ref[o] = out_ref[o] - 0.5 * product

    each_product(plan_ref, act)


def per_device(n_row, n_col, x_stack, s_stack, entries, counts):
    smem = pl.BlockSpec(memory_space=pltpu.SMEM)
    vmem = pl.BlockSpec(memory_space=pltpu.VMEM)
    hbm = pl.BlockSpec(memory_space=pltpu.HBM)
    params = pltpu.CompilerParams(vmem_limit_bytes=VMEM_LIMIT)
    piece = BS // n_row
    rows_out = CAP * piece + TABLE
    x_own = x_stack[0, 0]
    row_panel = lax.all_gather(x_stack[0], "col", axis=0, tiled=True).reshape(n_col * CAP, BS, BS)

    valid = jnp.arange(CAP, dtype=jnp.int32) < counts[0, 0]
    base = jnp.where(valid[:, None, None], 1.5 * x_own, 0.0)
    own = jnp.concatenate([entries.reshape(2 * CAP), counts.reshape(1), jnp.zeros((BS - 2 * CAP - 1,), jnp.int32)])
    slots = lax.all_to_all(jnp.broadcast_to(own[None, None], (n_col, 1, BS)), "col", 0, 0)
    cut = pl.pallas_call(
        functools.partial(cut_kernel, n_row),
        out_shape=jax.ShapeDtypeStruct((n_row * rows_out, BS), jnp.float32),
        in_specs=[vmem],
        out_specs=vmem,
        compiler_params=params,
        cost_estimate=pl.CostEstimate(flops=0, bytes_accessed=2**22, transcendentals=0),
        name="cut",
    )(s_stack[0, 0])
    packed = pl.pallas_call(
        functools.partial(pack_kernel, n_row, n_col),
        out_shape=jax.ShapeDtypeStruct((n_row * rows_out, BS), jnp.float32),
        in_specs=[vmem, vmem, pl.BlockSpec(memory_space=pl.ANY)],
        out_specs=vmem,
        compiler_params=params,
        name="pack",
    )(slots, cut, base)
    parts = rows_out // 2
    pieces = lax.all_to_all(packed.reshape(n_row, parts, 2, BS), "row", 0, 0).reshape(n_row * rows_out, BS)

    def select(*first):
        chosen, plan, most = pl.pallas_call(
            functools.partial(select_kernel, n_row, not first),
            out_shape=(
                jax.ShapeDtypeStruct((n_row * ROUND * piece, BS), jnp.float32),
                jax.ShapeDtypeStruct((8, BS), jnp.int32),
                jax.ShapeDtypeStruct((1, 1), jnp.int32),
            ),
            in_specs=[smem] * len(first) + [vmem],
            out_specs=(vmem, vmem, smem),
            compiler_params=params,
            name="select",
        )(*first, pieces)
        tiles = lax.all_to_all(chosen.reshape(n_row, ROUND * piece, BS), "row", 0, 0)
        return tiles.reshape(n_row * ROUND * piece, BS), plan, most[0, 0]

    def fetch(plan):
        return pl.pallas_call(
            fetch_kernel,
            out_shape=jax.ShapeDtypeStruct((AHEAD, BS, BS), jnp.float32),
            in_specs=[smem, hbm],
            out_specs=vmem,
            scratch_shapes=[pltpu.SemaphoreType.DMA((AHEAD,))],
            compiler_params=params,
            cost_estimate=pl.CostEstimate(flops=0, bytes_accessed=2**23, transcendentals=0),
            name="fetch",
        )(plan, row_panel)

    def multiply(tiles, plan, base, x_tiles):
        return pl.pallas_call(
            functools.partial(multiply_kernel, n_row),
            out_shape=jax.ShapeDtypeStruct((CAP, BS, BS), jnp.float32),
            in_specs=[smem, vmem, vmem, vmem, hbm],
            out_specs=vmem,
            scratch_shapes=[pltpu.VMEM((BS, BS), jnp.float32), pltpu.SemaphoreType.DMA],
            compiler_params=params,
            name="multiply",
        )(plan, base, tiles, x_tiles, row_panel)

    tiles, plan, most = select()

    def another(state):
        first, partial = state
        more, where, _ = select(first.reshape(1))
        return first + ROUND, multiply(more, where, partial, fetch(where))

    x_tiles = fetch(plan)
    result = lax.cond(
        most > ROUND,
        lambda ahead: lax.while_loop(
            lambda state: state[0] < most, another, (jnp.int32(ROUND), multiply(tiles, plan, base, ahead))
        )[1],
        lambda ahead: multiply(tiles, plan, base, ahead),
        x_tiles,
    )
    return result[None, None]


def solution(mesh):
    return jax.shard_map(
        functools.partial(per_device, mesh.shape["row"], mesh.shape["col"]),
        mesh=mesh,
        in_specs=(
            P("row", "col", None, None, None),
            P("row", "col", None, None, None),
            P("row", "col", None, None),
            P("row", "col"),
        ),
        out_specs=P("row", "col", None, None, None),
        check_vma=False,
    )
```

```python
import functools

import jax
import jax.numpy as jnp
from jax import lax
from jax.experimental import pallas as pl
from jax.experimental.pallas import tpu as pltpu
from jax.sharding import PartitionSpec as P

RB = 6
CB = 8
CAP = 4
BS = 128
ROUND = 12
AHEAD = 16
TABLE = 2

VMEM_LIMIT = 24 * 1024 * 1024


def iota(shape, dim):
    return lax.broadcasted_iota(jnp.int32, shape, dim)


def turned(i):
    out = 0
    for bit in range(5):
        out = out + lax.rem(lax.div(i, 2**bit), 2) * 2 ** (4 - bit)
    return out


def dot(a, b, dims=((1,), (0,))):
    return lax.dot_general(a, b, (dims, ((), ())), preferred_element_type=jnp.float32)


def split(a, parts):
    out = []
    for _ in range(parts):
        out.append(a.astype(jnp.bfloat16))
        a = a - out[-1].astype(jnp.float32)
    return out


def cut_kernel(n_row, s_ref, out_ref):
    piece = BS // n_row
    rows_out = CAP * piece + TABLE
    for e in range(CAP):
        for q in range(piece):
            out_ref[pl.ds(e * piece + q, n_row, stride=rows_out), :] = s_ref[e, q * n_row : (q + 1) * n_row, :]
    for t in range(TABLE):
        out_ref[pl.ds(CAP * piece + t, n_row, stride=rows_out), :] = jnp.zeros((n_row, BS), jnp.float32)


def pack_kernel(n_row, n_col, slots_ref, cut_ref, ahead_ref, out_ref):
    piece = BS // n_row
    rows_out = CAP * piece + TABLE
    out_ref[...] = cut_ref[...]
    of_slot = lax.rem(iota((BS, BS), 1), CAP)
    field = iota((BS, BS), 0)
    mine = iota((n_col, BS), 0) == lax.div(iota((n_col, BS), 1), CAP)
    got = slots_ref[...].reshape(n_col, BS).astype(jnp.float32)

    def along(at):
        spread = jnp.where(field == at, 1.0, 0.0)
        return jnp.sum(jnp.where(mine, dot(got, spread), 0.0), axis=0, keepdims=True)

    used = lax.rem(iota((1, BS), 1), CAP).astype(jnp.float32) < along(2 * CAP)
    block_row = jnp.where(used, along(of_slot), -1.0)
    block_col = along(of_slot + CAP)
    out_ref[pl.ds(CAP * piece, n_row, stride=rows_out), :] = jnp.broadcast_to(block_row, (n_row, BS))
    out_ref[pl.ds(CAP * piece + 1, n_row, stride=rows_out), :] = jnp.broadcast_to(block_col, (n_row, BS))


def select_kernel(n_row, initial, *refs):
    got_ref, out_ref, plan_ref, most_ref = refs[-4:]
    piece = BS // n_row
    rows_in = CAP * piece + TABLE
    base = CAP * piece
    slots = CAP * n_row
    my_row, my_col, first = turned(lax.axis_index("row")), lax.axis_index("col"), 0 if initial else refs[0][0]

    def strided(start):
        return got_ref[pl.ds(start, n_row, stride=rows_in), :]

    block_row, block_col = strided(base), strided(base + 1)
    lane = iota((n_row, BS), 1)
    own_row, own_col = [], []
    for o in range(CAP):
        here = lane == my_col * CAP + o
        own_row.append(jnp.sum(jnp.where(here, block_row, 0.0), axis=1, keepdims=True))
        own_col.append(jnp.sum(jnp.where(here, block_col, 0.0), axis=1, keepdims=True))
    both = jnp.concatenate([block_row, block_col], axis=0)
    of_slot, of_k = iota((BS, 2 * BS), 0), iota((BS, 2 * BS), 1)
    k = iota((n_row, 2 * BS), 1)
    within = lax.rem(k, CB).astype(jnp.float32)
    place = (lax.div(k, CB) * CAP + 1).astype(jnp.float32)
    spread = [dot(both, jnp.where(of_slot == lax.div(of_k, CB) * CAP + e, 1.0, 0.0)) for e in range(CAP)]
    in_col = [spread[e][n_row:] == within for e in range(CAP)]
    tables = []
    for o in range(CAP):
        wanted = jnp.where(own_row[o] < 0.0, -2.0, own_row[o])
        found = jnp.zeros((n_row, 2 * BS), jnp.float32)
        for e in range(CAP):
            found = jnp.where(in_col[e] & (spread[e][:n_row] == wanted), place + e, found)
        tables.append(found)
    table = jnp.concatenate(tables, axis=0)
    holds_row = jnp.concatenate(own_row, axis=0).astype(jnp.int32)
    holds_col = jnp.concatenate(own_col, axis=0).astype(jnp.int32)
    inner = turned(lax.rem(iota((slots, 1), 0), n_row)) * RB + holds_row
    valid = holds_row >= 0
    wide = iota((slots, BS), 1)
    at_head = jnp.where((wide == inner) & valid, 1.0, 0.0)
    at_tail = jnp.where((wide + BS == inner) & valid, 1.0, 0.0)
    of_col = jnp.where(wide == holds_col, 1.0, 0.0)
    nt = ((1,), (1,))
    m = (dot(table[:, :BS], at_head, nt) + dot(table[:, BS:], at_tail, nt)) * dot(of_col, of_col, nt)
    need = m[:n_row]
    for o in range(1, CAP):
        need = jnp.maximum(need, m[o * n_row : (o + 1) * n_row])
    need = jnp.where(need > 0.5, 1.0, 0.0)
    before = jnp.where(iota((slots, slots), 0) < iota((slots, slots), 1), 1.0, 0.0)
    rank = dot(need, before).astype(jnp.int32) - first
    rank = jnp.where(need > 0.5, rank, -1)
    chosen = jnp.concatenate([jnp.where(rank == p, 1.0, 0.0) for p in range(ROUND)], axis=0)
    rows = jnp.concatenate(
        [jnp.concatenate([strided(e * piece + q) for e in range(CAP)], axis=0) for q in range(piece)], axis=1
    )
    pick = jnp.concatenate([chosen.astype(jnp.bfloat16)] * 3, axis=1)
    part = dot(pick, jnp.concatenate(split(rows, 3), axis=0))
    for q in range(piece):
        for p in range(ROUND):
            out_ref[pl.ds(p * piece + q, n_row, stride=ROUND * piece), :] = part[
                p * n_row : (p + 1) * n_row, q * BS : (q + 1) * BS
            ]
    mine = iota((n_row, BS), 0) == my_row

    def own(a, n):
        return [jnp.sum(jnp.where(mine, a[i * n_row : (i + 1) * n_row], 0.0), axis=0, keepdims=True) for i in range(n)]

    own_m = jnp.concatenate(own(m, CAP) + [jnp.zeros((4, BS), jnp.float32)], axis=0)
    own_chosen = jnp.concatenate(own(chosen, ROUND) + [jnp.zeros((BS - ROUND, BS), jnp.float32)], axis=0)
    needed = jnp.sum(need, axis=1, keepdims=True)
    most_ref[0, 0] = (jnp.max(needed) + 0.5).astype(jnp.int32)
    here = jnp.sum(jnp.sum(own_chosen, axis=1, keepdims=True), axis=0, keepdims=True)
    plan = jnp.where(iota((8, BS), 0) == 7, here, dot(own_m, own_chosen, nt))
    plan_ref[...] = (plan + 0.5).astype(jnp.int32)


def each_product(plan_ref, act):
    def tile(p, n):
        for o in range(CAP):
            used = plan_ref[o, p] > 0

            @pl.when(used)
            def _():
                act(n, o, p)

            n = n + used.astype(jnp.int32)
        return n

    lax.fori_loop(0, plan_ref[7, 0], tile, 0)


def fetch_kernel(plan_ref, x_ref, out_ref, sems):
    def copy(n, o, p):
        return pltpu.make_async_copy(x_ref.at[plan_ref[o, p] - 1], out_ref.at[n], sems.at[n])

    def start(n, o, p):
        @pl.when(n < AHEAD)
        def _():
            copy(n, o, p).start()

    def wait(n, o, p):
        @pl.when(n < AHEAD)
        def _():
            copy(n, o, p).wait()

    each_product(plan_ref, start)
    each_product(plan_ref, wait)


def multiply_kernel(n_row, plan_ref, base_ref, got_ref, ahead_ref, x_ref, out_ref, x_buf, sem):
    piece = BS // n_row
    out_ref[...] = base_ref[...]

    def act(n, o, p):
        s_tile = jnp.concatenate(
            [got_ref[pl.ds(p * piece + q, n_row, stride=ROUND * piece), :] for q in range(piece)], axis=0
        )
        s_high, s_low = split(s_tile, 2)

        @pl.when(n < AHEAD)
        def _():
            x_buf[...] = ahead_ref[jnp.minimum(n, AHEAD - 1)]

        @pl.when(n >= AHEAD)
        def _():
            copy = pltpu.make_async_copy(x_ref.at[plan_ref[o, p] - 1], x_buf, sem)
            copy.start()
            copy.wait()

        x_high, x_low = split(x_buf[...], 2)
        product = dot(x_high, s_high) + (dot(x_high, s_low) + dot(x_low, s_high))
        out_ref[o] = out_ref[o] - 0.5 * product

    each_product(plan_ref, act)


def per_device(n_row, n_col, x_stack, s_stack, entries, counts):
    smem = pl.BlockSpec(memory_space=pltpu.SMEM)
    vmem = pl.BlockSpec(memory_space=pltpu.VMEM)
    hbm = pl.BlockSpec(memory_space=pltpu.HBM)
    params = pltpu.CompilerParams(vmem_limit_bytes=VMEM_LIMIT)
    piece = BS // n_row
    rows_out = CAP * piece + TABLE
    x_own = x_stack[0, 0]
    row_panel = lax.all_gather(x_stack[0], "col", axis=0, tiled=True).reshape(n_col * CAP, BS, BS)

    valid = jnp.arange(CAP, dtype=jnp.int32) < counts[0, 0]
    base = jnp.where(valid[:, None, None], 1.5 * x_own, 0.0)
    own = jnp.concatenate([entries.reshape(2 * CAP), counts.reshape(1), jnp.zeros((BS - 2 * CAP - 1,), jnp.int32)])
    slots = lax.all_to_all(jnp.broadcast_to(own[None, None], (n_col, 1, BS)), "col", 0, 0)
    cut = pl.pallas_call(
        functools.partial(cut_kernel, n_row),
        out_shape=jax.ShapeDtypeStruct((n_row * rows_out, BS), jnp.float32),
        in_specs=[vmem],
        out_specs=vmem,
        compiler_params=params,
        cost_estimate=pl.CostEstimate(flops=0, bytes_accessed=2**22, transcendentals=0),
        name="cut",
    )(s_stack[0, 0])
    packed = pl.pallas_call(
        functools.partial(pack_kernel, n_row, n_col),
        out_shape=jax.ShapeDtypeStruct((n_row * rows_out, BS), jnp.float32),
        in_specs=[vmem, vmem, pl.BlockSpec(memory_space=pl.ANY)],
        out_specs=vmem,
        compiler_params=params,
        name="pack",
    )(slots, cut, base)
    parts = rows_out // 2
    pieces = lax.all_to_all(packed.reshape(n_row, parts, 2, BS), "row", 0, 0, axis_index_groups=[[int(format(i, "05b")[::-1], 2) for i in range(n_row)]]).reshape(n_row * rows_out, BS)

    def select(*first):
        chosen, plan, most = pl.pallas_call(
            functools.partial(select_kernel, n_row, not first),
            out_shape=(
                jax.ShapeDtypeStruct((n_row * ROUND * piece, BS), jnp.float32),
                jax.ShapeDtypeStruct((8, BS), jnp.int32),
                jax.ShapeDtypeStruct((1, 1), jnp.int32),
            ),
            in_specs=[smem] * len(first) + [vmem],
            out_specs=(vmem, vmem, smem),
            compiler_params=params,
            name="select",
        )(*first, pieces)
        tiles = lax.all_to_all(chosen.reshape(n_row, ROUND * piece, BS), "row", 0, 0, axis_index_groups=[[int(format(i, "05b")[::-1], 2) for i in range(n_row)]])
        return tiles.reshape(n_row * ROUND * piece, BS), plan, most[0, 0]

    def fetch(plan):
        return pl.pallas_call(
            fetch_kernel,
            out_shape=jax.ShapeDtypeStruct((AHEAD, BS, BS), jnp.float32),
            in_specs=[smem, hbm],
            out_specs=vmem,
            scratch_shapes=[pltpu.SemaphoreType.DMA((AHEAD,))],
            compiler_params=params,
            cost_estimate=pl.CostEstimate(flops=0, bytes_accessed=2**23, transcendentals=0),
            name="fetch",
        )(plan, row_panel)

    def multiply(tiles, plan, base, x_tiles):
        return pl.pallas_call(
            functools.partial(multiply_kernel, n_row),
            out_shape=jax.ShapeDtypeStruct((CAP, BS, BS), jnp.float32),
            in_specs=[smem, vmem, vmem, vmem, hbm],
            out_specs=vmem,
            scratch_shapes=[pltpu.VMEM((BS, BS), jnp.float32), pltpu.SemaphoreType.DMA],
            compiler_params=params,
            name="multiply",
        )(plan, base, tiles, x_tiles, row_panel)

    tiles, plan, most = select()

    def another(state):
        first, partial = state
        more, where, _ = select(first.reshape(1))
        return first + ROUND, multiply(more, where, partial, fetch(where))

    x_tiles = fetch(plan)
    result = lax.cond(
        most > ROUND,
        lambda ahead: lax.while_loop(
            lambda state: state[0] < most, another, (jnp.int32(ROUND), multiply(tiles, plan, base, ahead))
        )[1],
        lambda ahead: multiply(tiles, plan, base, ahead),
        x_tiles,
    )
    return result[None, None]


def solution(mesh):
    return jax.shard_map(
        functools.partial(per_device, mesh.shape["row"], mesh.shape["col"]),
        mesh=mesh,
        in_specs=(
            P("row", "col", None, None, None),
            P("row", "col", None, None, None),
            P("row", "col", None, None),
            P("row", "col"),
        ),
        out_specs=P("row", "col", None, None, None),
        check_vma=False,
    )
```

```python
import functools

import jax
import jax.numpy as jnp
from jax import lax
from jax.experimental import pallas as pl
from jax.experimental.pallas import tpu as pltpu
from jax.sharding import PartitionSpec as P

RB = 6
CB = 8
CAP = 4
BS = 128
ROUND = 12
AHEAD = 16
TABLE = 2

VMEM_LIMIT = 24 * 1024 * 1024


def iota(shape, dim):
    return lax.broadcasted_iota(jnp.int32, shape, dim)


def turned(i):
    out = 0
    for bit in range(5):
        out = out + lax.rem(lax.div(i, 2**bit), 2) * 2 ** (4 - bit)
    return out


def dot(a, b, dims=((1,), (0,))):
    return lax.dot_general(a, b, (dims, ((), ())), preferred_element_type=jnp.float32)


def split(a, parts):
    out = []
    for _ in range(parts):
        out.append(a.astype(jnp.bfloat16))
        a = a - out[-1].astype(jnp.float32)
    return out


def cut_kernel(n_row, s_ref, out_ref):
    piece = BS // n_row
    rows_out = CAP * piece + TABLE
    for e in range(CAP):
        for q in range(piece):
            out_ref[pl.ds(e * piece + q, n_row, stride=rows_out), :] = s_ref[e, q * n_row : (q + 1) * n_row, :]
    for t in range(TABLE):
        out_ref[pl.ds(CAP * piece + t, n_row, stride=rows_out), :] = jnp.zeros((n_row, BS), jnp.float32)


def pack_kernel(n_row, n_col, slots_ref, cut_ref, ahead_ref, out_ref):
    piece = BS // n_row
    rows_out = CAP * piece + TABLE
    out_ref[...] = cut_ref[...]
    of_slot = lax.rem(iota((BS, BS), 1), CAP)
    field = iota((BS, BS), 0)
    mine = iota((n_col, BS), 0) == lax.div(iota((n_col, BS), 1), CAP)
    got = slots_ref[...].reshape(n_col, BS).astype(jnp.float32)

    def along(at):
        spread = jnp.where(field == at, 1.0, 0.0)
        return jnp.sum(jnp.where(mine, dot(got, spread), 0.0), axis=0, keepdims=True)

    used = lax.rem(iota((1, BS), 1), CAP).astype(jnp.float32) < along(2 * CAP)
    block_row = jnp.where(used, along(of_slot), -1.0)
    block_col = along(of_slot + CAP)
    out_ref[pl.ds(CAP * piece, n_row, stride=rows_out), :] = jnp.broadcast_to(block_row, (n_row, BS))
    out_ref[pl.ds(CAP * piece + 1, n_row, stride=rows_out), :] = jnp.broadcast_to(block_col, (n_row, BS))


def select_kernel(n_row, initial, *refs):
    got_ref, out_ref, plan_ref, most_ref = refs[-4:]
    piece = BS // n_row
    rows_in = CAP * piece + TABLE
    base = CAP * piece
    slots = CAP * n_row
    my_row, my_col, first = turned(lax.axis_index("row")), lax.axis_index("col"), 0 if initial else refs[0][0]

    def strided(start):
        return got_ref[pl.ds(start, n_row, stride=rows_in), :]

    block_row, block_col = strided(base), strided(base + 1)
    lane = iota((n_row, BS), 1)
    own_row, own_col = [], []
    for o in range(CAP):
        here = lane == my_col * CAP + o
        own_row.append(jnp.sum(jnp.where(here, block_row, 0.0), axis=1, keepdims=True))
        own_col.append(jnp.sum(jnp.where(here, block_col, 0.0), axis=1, keepdims=True))
    both = jnp.concatenate([block_row, block_col], axis=0)
    of_slot, of_k = iota((BS, 2 * BS), 0), iota((BS, 2 * BS), 1)
    k = iota((n_row, 2 * BS), 1)
    within = lax.rem(k, CB).astype(jnp.float32)
    place = (lax.div(k, CB) * CAP + 1).astype(jnp.float32)
    spread = [dot(both, jnp.where(of_slot == lax.div(of_k, CB) * CAP + e, 1.0, 0.0)) for e in range(CAP)]
    in_col = [spread[e][n_row:] == within for e in range(CAP)]
    tables = []
    for o in range(CAP):
        wanted = jnp.where(own_row[o] < 0.0, -2.0, own_row[o])
        found = jnp.zeros((n_row, 2 * BS), jnp.float32)
        for e in range(CAP):
            found = jnp.where(in_col[e] & (spread[e][:n_row] == wanted), place + e, found)
        tables.append(found)
    table = jnp.concatenate(tables, axis=0)
    holds_row = jnp.concatenate(own_row, axis=0).astype(jnp.int32)
    holds_col = jnp.concatenate(own_col, axis=0).astype(jnp.int32)
    inner = turned(lax.rem(iota((slots, 1), 0), n_row)) * RB + holds_row
    valid = holds_row >= 0
    wide = iota((slots, BS), 1)
    at_head = jnp.where((wide == inner) & valid, 1.0, 0.0)
    at_tail = jnp.where((wide + BS == inner) & valid, 1.0, 0.0)
    of_col = jnp.where(wide == holds_col, 1.0, 0.0)
    nt = ((1,), (1,))
    m = (dot(table[:, :BS], at_head, nt) + dot(table[:, BS:], at_tail, nt)) * dot(of_col, of_col, nt)
    need = m[:n_row]
    for o in range(1, CAP):
        need = jnp.maximum(need, m[o * n_row : (o + 1) * n_row])
    need = jnp.where(need > 0.5, 1.0, 0.0)
    before = jnp.where(iota((slots, slots), 0) < iota((slots, slots), 1), 1.0, 0.0)
    rank = dot(need, before).astype(jnp.int32) - first
    rank = jnp.where(need > 0.5, rank, -1)
    chosen = jnp.concatenate([jnp.where(rank == p, 1.0, 0.0) for p in range(ROUND)], axis=0)
    rows = jnp.concatenate(
        [jnp.concatenate([strided(e * piece + q) for e in range(CAP)], axis=0) for q in range(piece)], axis=1
    )
    pick = jnp.concatenate([chosen.astype(jnp.bfloat16)] * 2, axis=1)
    part = dot(pick, jnp.concatenate(split(rows, 2), axis=0))
    for q in range(piece):
        for p in range(ROUND):
            out_ref[pl.ds(p * piece + q, n_row, stride=ROUND * piece), :] = part[
                p * n_row : (p + 1) * n_row, q * BS : (q + 1) * BS
            ]
    mine = iota((n_row, BS), 0) == my_row

    def own(a, n):
        return [jnp.sum(jnp.where(mine, a[i * n_row : (i + 1) * n_row], 0.0), axis=0, keepdims=True) for i in range(n)]

    own_m = jnp.concatenate(own(m, CAP) + [jnp.zeros((4, BS), jnp.float32)], axis=0)
    own_chosen = jnp.concatenate(own(chosen, ROUND) + [jnp.zeros((BS - ROUND, BS), jnp.float32)], axis=0)
    needed = jnp.sum(need, axis=1, keepdims=True)
    most_ref[0, 0] = (jnp.max(needed) + 0.5).astype(jnp.int32)
    here = jnp.sum(jnp.sum(own_chosen, axis=1, keepdims=True), axis=0, keepdims=True)
    plan = jnp.where(iota((8, BS), 0) == 7, here, dot(own_m, own_chosen, nt))
    plan_ref[...] = (plan + 0.5).astype(jnp.int32)


def each_product(plan_ref, act):
    def tile(p, n):
        for o in range(CAP):
            used = plan_ref[o, p] > 0

            @pl.when(used)
            def _():
                act(n, o, p)

            n = n + used.astype(jnp.int32)
        return n

    return lax.fori_loop(0, plan_ref[7, 0], tile, 0)


def fetch_kernel(plan_ref, x_ref, out_ref, sems):
    def copy(n, o, p):
        return pltpu.make_async_copy(x_ref.at[plan_ref[o, p] - 1], out_ref.at[n], sems.at[n])

    def start(n, o, p):
        @pl.when(n < AHEAD)
        def _():
            copy(n, o, p).start()

    started = each_product(plan_ref, start)

    @pl.loop(0, jnp.minimum(started, AHEAD))
    def _(n):
        pltpu.make_async_copy(x_ref.at[0], out_ref.at[n], sems.at[n]).wait()


def multiply_kernel(n_row, plan_ref, base_ref, got_ref, ahead_ref, x_ref, out_ref, x_buf, sem):
    piece = BS // n_row
    out_ref[...] = base_ref[...]

    def act(n, o, p):
        s_tile = jnp.concatenate(
            [got_ref[pl.ds(p * piece + q, n_row, stride=ROUND * piece), :] for q in range(piece)], axis=0
        )
        s_high, s_low = split(s_tile, 2)

        @pl.when(n < AHEAD)
        def _():
            x_buf[...] = ahead_ref[jnp.minimum(n, AHEAD - 1)]

        @pl.when(n >= AHEAD)
        def _():
            copy = pltpu.make_async_copy(x_ref.at[plan_ref[o, p] - 1], x_buf, sem)
            copy.start()
            copy.wait()

        x_high, x_low = split(x_buf[...], 2)
        product = dot(x_high, s_high) + (dot(x_high, s_low) + dot(x_low, s_high))
        out_ref[o] = out_ref[o] - 0.5 * product

    each_product(plan_ref, act)


def per_device(n_row, n_col, x_stack, s_stack, entries, counts):
    smem = pl.BlockSpec(memory_space=pltpu.SMEM)
    vmem = pl.BlockSpec(memory_space=pltpu.VMEM)
    hbm = pl.BlockSpec(memory_space=pltpu.HBM)
    params = pltpu.CompilerParams(vmem_limit_bytes=VMEM_LIMIT)
    piece = BS // n_row
    rows_out = CAP * piece + TABLE
    x_own = x_stack[0, 0]
    row_panel = lax.all_gather(x_stack[0], "col", axis=0, tiled=True).reshape(n_col * CAP, BS, BS)

    valid = jnp.arange(CAP, dtype=jnp.int32) < counts[0, 0]
    base = jnp.where(valid[:, None, None], 1.5 * x_own, 0.0)
    own = jnp.concatenate([entries.reshape(2 * CAP), counts.reshape(1), jnp.zeros((BS - 2 * CAP - 1,), jnp.int32)])
    slots = lax.all_to_all(jnp.broadcast_to(own[None, None], (n_col, 1, BS)), "col", 0, 0)
    cut = pl.pallas_call(
        functools.partial(cut_kernel, n_row),
        out_shape=jax.ShapeDtypeStruct((n_row * rows_out, BS), jnp.float32),
        in_specs=[vmem],
        out_specs=vmem,
        compiler_params=params,
        cost_estimate=pl.CostEstimate(flops=0, bytes_accessed=2**22, transcendentals=0),
        name="cut",
    )(s_stack[0, 0])
    packed = pl.pallas_call(
        functools.partial(pack_kernel, n_row, n_col),
        out_shape=jax.ShapeDtypeStruct((n_row * rows_out, BS), jnp.float32),
        in_specs=[vmem, vmem, pl.BlockSpec(memory_space=pl.ANY)],
        out_specs=vmem,
        compiler_params=params,
        name="pack",
    )(slots, cut, base)
    parts = rows_out // 2
    pieces = lax.all_to_all(packed.reshape(n_row, parts, 2, BS), "row", 0, 0, axis_index_groups=[[int(format(i, "05b")[::-1], 2) for i in range(n_row)]]).reshape(n_row * rows_out, BS)

    def select(*first):
        chosen, plan, most = pl.pallas_call(
            functools.partial(select_kernel, n_row, not first),
            out_shape=(
                jax.ShapeDtypeStruct((n_row * ROUND * piece, BS), jnp.float32),
                jax.ShapeDtypeStruct((8, BS), jnp.int32),
                jax.ShapeDtypeStruct((1, 1), jnp.int32),
            ),
            in_specs=[smem] * len(first) + [vmem],
            out_specs=(vmem, vmem, smem),
            compiler_params=params,
            name="select",
        )(*first, pieces)
        tiles = lax.all_to_all(chosen.reshape(n_row, ROUND * piece, BS), "row", 0, 0, axis_index_groups=[[int(format(i, "05b")[::-1], 2) for i in range(n_row)]])
        return tiles.reshape(n_row * ROUND * piece, BS), plan, most[0, 0]

    def fetch(plan):
        return pl.pallas_call(
            fetch_kernel,
            out_shape=jax.ShapeDtypeStruct((AHEAD, BS, BS), jnp.float32),
            in_specs=[smem, hbm],
            out_specs=vmem,
            scratch_shapes=[pltpu.SemaphoreType.DMA((AHEAD,))],
            compiler_params=params,
            cost_estimate=pl.CostEstimate(flops=0, bytes_accessed=2**23, transcendentals=0),
            name="fetch",
        )(plan, row_panel)

    def multiply(tiles, plan, base, x_tiles):
        return pl.pallas_call(
            functools.partial(multiply_kernel, n_row),
            out_shape=jax.ShapeDtypeStruct((CAP, BS, BS), jnp.float32),
            in_specs=[smem, vmem, vmem, vmem, hbm],
            out_specs=vmem,
            scratch_shapes=[pltpu.VMEM((BS, BS), jnp.float32), pltpu.SemaphoreType.DMA],
            compiler_params=params,
            name="multiply",
        )(plan, base, tiles, x_tiles, row_panel)

    tiles, plan, most = select()

    def another(state):
        first, partial = state
        more, where, _ = select(first.reshape(1))
        return first + ROUND, multiply(more, where, partial, fetch(where))

    x_tiles = fetch(plan)
    result = lax.cond(
        most > ROUND,
        lambda ahead: lax.while_loop(
            lambda state: state[0] < most, another, (jnp.int32(ROUND), multiply(tiles, plan, base, ahead))
        )[1],
        lambda ahead: multiply(tiles, plan, base, ahead),
        x_tiles,
    )
    return result[None, None]


def solution(mesh):
    return jax.shard_map(
        functools.partial(per_device, mesh.shape["row"], mesh.shape["col"]),
        mesh=mesh,
        in_specs=(
            P("row", "col", None, None, None),
            P("row", "col", None, None, None),
            P("row", "col", None, None),
            P("row", "col"),
        ),
        out_specs=P("row", "col", None, None, None),
        check_vma=False,
    )
```

```python
import functools

import jax
import jax.numpy as jnp
from jax import lax
from jax.experimental import pallas as pl
from jax.experimental.pallas import tpu as pltpu
from jax.sharding import PartitionSpec as P

RB = 6
CB = 8
CAP = 4
BS = 128
ROUND = 12
AHEAD = 16
TABLE = 2

VMEM_LIMIT = 24 * 1024 * 1024


def iota(shape, dim):
    return lax.broadcasted_iota(jnp.int32, shape, dim)


def turned(i):
    out = 0
    for bit in range(5):
        out = out + lax.rem(lax.div(i, 2**bit), 2) * 2 ** (4 - bit)
    return out


def dot(a, b, dims=((1,), (0,))):
    return lax.dot_general(a, b, (dims, ((), ())), preferred_element_type=jnp.float32)


def split(a, parts):
    out = []
    for _ in range(parts):
        out.append(a.astype(jnp.bfloat16))
        a = a - out[-1].astype(jnp.float32)
    return out


def cut_kernel(n_row, s_ref, out_ref):
    piece = BS // n_row
    rows_out = CAP * piece + TABLE
    for e in range(CAP):
        for q in range(piece):
            for i in range(n_row):
                at = int(format(i, "05b")[::-1], 2) * rows_out + e * piece + q
                out_ref[at : at + 1, :] = s_ref[e, q * n_row + i : q * n_row + i + 1, :]
    for t in range(TABLE):
        out_ref[pl.ds(CAP * piece + t, n_row, stride=rows_out), :] = jnp.zeros((n_row, BS), jnp.float32)


def pack_kernel(n_row, n_col, slots_ref, cut_ref, ahead_ref, out_ref):
    piece = BS // n_row
    rows_out = CAP * piece + TABLE
    out_ref[...] = cut_ref[...]
    of_slot = lax.rem(iota((BS, BS), 1), CAP)
    field = iota((BS, BS), 0)
    mine = iota((n_col, BS), 0) == lax.div(iota((n_col, BS), 1), CAP)
    got = slots_ref[...].reshape(n_col, BS).astype(jnp.float32)

    def along(at):
        spread = jnp.where(field == at, 1.0, 0.0)
        return jnp.sum(jnp.where(mine, dot(got, spread), 0.0), axis=0, keepdims=True)

    used = lax.rem(iota((1, BS), 1), CAP).astype(jnp.float32) < along(2 * CAP)
    block_row = jnp.where(used, along(of_slot), -1.0)
    block_col = along(of_slot + CAP)
    out_ref[pl.ds(CAP * piece, n_row, stride=rows_out), :] = jnp.broadcast_to(block_row, (n_row, BS))
    out_ref[pl.ds(CAP * piece + 1, n_row, stride=rows_out), :] = jnp.broadcast_to(block_col, (n_row, BS))


def select_kernel(n_row, initial, *refs):
    got_ref, out_ref, plan_ref, most_ref = refs[-4:]
    piece = BS // n_row
    rows_in = CAP * piece + TABLE
    base = CAP * piece
    slots = CAP * n_row
    my_row, my_col, first = lax.axis_index("row"), lax.axis_index("col"), 0 if initial else refs[0][0]

    def strided(start):
        return got_ref[pl.ds(start, n_row, stride=rows_in), :]

    block_row, block_col = strided(base), strided(base + 1)
    lane = iota((n_row, BS), 1)
    own_row, own_col = [], []
    for o in range(CAP):
        here = lane == my_col * CAP + o
        own_row.append(jnp.sum(jnp.where(here, block_row, 0.0), axis=1, keepdims=True))
        own_col.append(jnp.sum(jnp.where(here, block_col, 0.0), axis=1, keepdims=True))
    both = jnp.concatenate([block_row, block_col], axis=0)
    of_slot, of_k = iota((BS, 2 * BS), 0), iota((BS, 2 * BS), 1)
    k = iota((n_row, 2 * BS), 1)
    within = lax.rem(k, CB).astype(jnp.float32)
    place = (lax.div(k, CB) * CAP + 1).astype(jnp.float32)
    spread = [dot(both, jnp.where(of_slot == lax.div(of_k, CB) * CAP + e, 1.0, 0.0)) for e in range(CAP)]
    in_col = [spread[e][n_row:] == within for e in range(CAP)]
    tables = []
    for o in range(CAP):
        wanted = jnp.where(own_row[o] < 0.0, -2.0, own_row[o])
        found = jnp.zeros((n_row, 2 * BS), jnp.float32)
        for e in range(CAP):
            found = jnp.where(in_col[e] & (spread[e][:n_row] == wanted), place + e, found)
        tables.append(found)
    table = jnp.concatenate(tables, axis=0)
    holds_row = jnp.concatenate(own_row, axis=0).astype(jnp.int32)
    holds_col = jnp.concatenate(own_col, axis=0).astype(jnp.int32)
    inner = lax.rem(iota((slots, 1), 0), n_row) * RB + holds_row
    valid = holds_row >= 0
    wide = iota((slots, BS), 1)
    at_head = jnp.where((wide == inner) & valid, 1.0, 0.0)
    at_tail = jnp.where((wide + BS == inner) & valid, 1.0, 0.0)
    of_col = jnp.where(wide == holds_col, 1.0, 0.0)
    nt = ((1,), (1,))
    m = (dot(table[:, :BS], at_head, nt) + dot(table[:, BS:], at_tail, nt)) * dot(of_col, of_col, nt)
    need = m[:n_row]
    for o in range(1, CAP):
        need = jnp.maximum(need, m[o * n_row : (o + 1) * n_row])
    need = jnp.where(need > 0.5, 1.0, 0.0)
    before = jnp.where(iota((slots, slots), 0) < iota((slots, slots), 1), 1.0, 0.0)
    rank = dot(need, before).astype(jnp.int32) - first
    rank = jnp.where(need > 0.5, rank, -1)
    order = jnp.where(iota((n_row, n_row), 1) == turned(iota((n_row, n_row), 0)), 1.0, 0.0)
    rank = dot(order, rank.astype(jnp.float32)).astype(jnp.int32)
    chosen = jnp.concatenate([jnp.where(rank == p, 1.0, 0.0) for p in range(ROUND)], axis=0)
    rows = jnp.concatenate(
        [jnp.concatenate([strided(e * piece + q) for e in range(CAP)], axis=0) for q in range(piece)], axis=1
    )
    pick = jnp.concatenate([chosen.astype(jnp.bfloat16)] * 2, axis=1)
    part = dot(pick, jnp.concatenate(split(rows, 2), axis=0))
    for q in range(piece):
        for p in range(ROUND):
            out_ref[pl.ds(p * piece + q, n_row, stride=ROUND * piece), :] = part[
                p * n_row : (p + 1) * n_row, q * BS : (q + 1) * BS
            ]

    def own(a, n, at):
        return [jnp.sum(jnp.where(iota((n_row, BS), 0) == at, a[i * n_row : (i + 1) * n_row], 0.0), axis=0, keepdims=True) for i in range(n)]

    own_m = jnp.concatenate(own(m, CAP, my_row) + [jnp.zeros((4, BS), jnp.float32)], axis=0)
    own_chosen = jnp.concatenate(own(chosen, ROUND, turned(my_row)) + [jnp.zeros((BS - ROUND, BS), jnp.float32)], axis=0)
    needed = jnp.sum(need, axis=1, keepdims=True)
    most_ref[0, 0] = (jnp.max(needed) + 0.5).astype(jnp.int32)
    here = jnp.sum(jnp.sum(own_chosen, axis=1, keepdims=True), axis=0, keepdims=True)
    plan = jnp.where(iota((8, BS), 0) == 7, here, dot(own_m, own_chosen, nt))
    plan_ref[...] = (plan + 0.5).astype(jnp.int32)


def each_product(plan_ref, act):
    def tile(p, n):
        for o in range(CAP):
            used = plan_ref[o, p] > 0

            @pl.when(used)
            def _():
                act(n, o, p)

            n = n + used.astype(jnp.int32)
        return n

    return lax.fori_loop(0, plan_ref[7, 0], tile, 0)


def fetch_kernel(plan_ref, x_ref, out_ref, sems):
    def copy(n, o, p):
        return pltpu.make_async_copy(x_ref.at[plan_ref[o, p] - 1], out_ref.at[n], sems.at[n])

    def start(n, o, p):
        @pl.when(n < AHEAD)
        def _():
            copy(n, o, p).start()

    started = each_product(plan_ref, start)

    @pl.loop(0, jnp.minimum(started, AHEAD))
    def _(n):
        pltpu.make_async_copy(x_ref.at[0], out_ref.at[n], sems.at[n]).wait()


def multiply_kernel(n_row, plan_ref, base_ref, got_ref, ahead_ref, x_ref, out_ref, x_buf, sem):
    piece = BS // n_row
    out_ref[...] = base_ref[...]

    def act(n, o, p):
        s_tile = jnp.concatenate(
            [got_ref[pl.ds(p * piece + q, n_row, stride=ROUND * piece), :] for q in range(piece)], axis=0
        )
        s_high, s_low = split(s_tile, 2)

        @pl.when(n < AHEAD)
        def _():
            x_buf[...] = ahead_ref[jnp.minimum(n, AHEAD - 1)]

        @pl.when(n >= AHEAD)
        def _():
            copy = pltpu.make_async_copy(x_ref.at[plan_ref[o, p] - 1], x_buf, sem)
            copy.start()
            copy.wait()

        x_high, x_low = split(x_buf[...], 2)
        product = dot(x_high, s_high) + (dot(x_high, s_low) + dot(x_low, s_high))
        out_ref[o] = out_ref[o] - 0.5 * product

    each_product(plan_ref, act)


def per_device(n_row, n_col, x_stack, s_stack, entries, counts):
    smem = pl.BlockSpec(memory_space=pltpu.SMEM)
    vmem = pl.BlockSpec(memory_space=pltpu.VMEM)
    hbm = pl.BlockSpec(memory_space=pltpu.HBM)
    params = pltpu.CompilerParams(vmem_limit_bytes=VMEM_LIMIT)
    piece = BS // n_row
    rows_out = CAP * piece + TABLE
    x_own = x_stack[0, 0]
    row_panel = lax.all_gather(x_stack[0], "col", axis=0, tiled=True).reshape(n_col * CAP, BS, BS)

    valid = jnp.arange(CAP, dtype=jnp.int32) < counts[0, 0]
    base = jnp.where(valid[:, None, None], 1.5 * x_own, 0.0)
    own = jnp.concatenate([entries.reshape(2 * CAP), counts.reshape(1), jnp.zeros((BS - 2 * CAP - 1,), jnp.int32)])
    slots = lax.all_to_all(jnp.broadcast_to(own[None, None], (n_col, 1, BS)), "col", 0, 0)
    cut = pl.pallas_call(
        functools.partial(cut_kernel, n_row),
        out_shape=jax.ShapeDtypeStruct((n_row * rows_out, BS), jnp.float32),
        in_specs=[vmem],
        out_specs=vmem,
        compiler_params=params,
        cost_estimate=pl.CostEstimate(flops=0, bytes_accessed=2**22, transcendentals=0),
        name="cut",
    )(s_stack[0, 0])
    packed = pl.pallas_call(
        functools.partial(pack_kernel, n_row, n_col),
        out_shape=jax.ShapeDtypeStruct((n_row * rows_out, BS), jnp.float32),
        in_specs=[vmem, vmem, pl.BlockSpec(memory_space=pl.ANY)],
        out_specs=vmem,
        compiler_params=params,
        name="pack",
    )(slots, cut, base)
    parts = rows_out // 2
    pieces = lax.all_to_all(packed.reshape(n_row, parts, 2, BS), "row", 0, 0).reshape(n_row * rows_out, BS)

    def select(*first):
        chosen, plan, most = pl.pallas_call(
            functools.partial(select_kernel, n_row, not first),
            out_shape=(
                jax.ShapeDtypeStruct((n_row * ROUND * piece, BS), jnp.float32),
                jax.ShapeDtypeStruct((8, BS), jnp.int32),
                jax.ShapeDtypeStruct((1, 1), jnp.int32),
            ),
            in_specs=[smem] * len(first) + [vmem],
            out_specs=(vmem, vmem, smem),
            compiler_params=params,
            name="select",
        )(*first, pieces)
        tiles = lax.all_to_all(chosen.reshape(n_row, ROUND * piece, BS), "row", 0, 0, axis_index_groups=[[int(format(i, "05b")[::-1], 2) for i in range(n_row)]])
        return tiles.reshape(n_row * ROUND * piece, BS), plan, most[0, 0]

    def fetch(plan):
        return pl.pallas_call(
            fetch_kernel,
            out_shape=jax.ShapeDtypeStruct((AHEAD, BS, BS), jnp.float32),
            in_specs=[smem, hbm],
            out_specs=vmem,
            scratch_shapes=[pltpu.SemaphoreType.DMA((AHEAD,))],
            compiler_params=params,
            cost_estimate=pl.CostEstimate(flops=0, bytes_accessed=2**23, transcendentals=0),
            name="fetch",
        )(plan, row_panel)

    def multiply(tiles, plan, base, x_tiles):
        return pl.pallas_call(
            functools.partial(multiply_kernel, n_row),
            out_shape=jax.ShapeDtypeStruct((CAP, BS, BS), jnp.float32),
            in_specs=[smem, vmem, vmem, vmem, hbm],
            out_specs=vmem,
            scratch_shapes=[pltpu.VMEM((BS, BS), jnp.float32), pltpu.SemaphoreType.DMA],
            compiler_params=params,
            name="multiply",
        )(plan, base, tiles, x_tiles, row_panel)

    tiles, plan, most = select()

    def another(state):
        first, partial = state
        more, where, _ = select(first.reshape(1))
        return first + ROUND, multiply(more, where, partial, fetch(where))

    x_tiles = fetch(plan)
    result = lax.cond(
        most > ROUND,
        lambda ahead: lax.while_loop(
            lambda state: state[0] < most, another, (jnp.int32(ROUND), multiply(tiles, plan, base, ahead))
        )[1],
        lambda ahead: multiply(tiles, plan, base, ahead),
        x_tiles,
    )
    return result[None, None]


def solution(mesh):
    return jax.shard_map(
        functools.partial(per_device, mesh.shape["row"], mesh.shape["col"]),
        mesh=mesh,
        in_specs=(
            P("row", "col", None, None, None),
            P("row", "col", None, None, None),
            P("row", "col", None, None),
            P("row", "col"),
        ),
        out_specs=P("row", "col", None, None, None),
        check_vma=False,
    )
```

```python
import functools

import jax
import jax.numpy as jnp
from jax import lax
from jax.experimental import pallas as pl
from jax.experimental.pallas import tpu as pltpu
from jax.sharding import PartitionSpec as P

RB = 6
CB = 8
CAP = 4
BS = 128
ROUND = 12
AHEAD = 16
TABLE = 2

VMEM_LIMIT = 24 * 1024 * 1024


def iota(shape, dim):
    return lax.broadcasted_iota(jnp.int32, shape, dim)


def turned(i):
    out = 0
    for bit in range(5):
        out = out + lax.rem(lax.div(i, 2**bit), 2) * 2 ** (4 - bit)
    return out


def dot(a, b, dims=((1,), (0,))):
    return lax.dot_general(a, b, (dims, ((), ())), preferred_element_type=jnp.float32)


def split(a, parts):
    out = []
    for _ in range(parts):
        out.append(a.astype(jnp.bfloat16))
        a = a - out[-1].astype(jnp.float32)
    return out


def cut_kernel(n_row, s_ref, out_ref):
    piece = BS // n_row
    rows_out = CAP * piece + TABLE
    for e in range(CAP):
        for q in range(piece):
            out_ref[pl.ds(e * piece + q, n_row, stride=rows_out), :] = s_ref[e, q * n_row : (q + 1) * n_row, :]
    for t in range(TABLE):
        out_ref[pl.ds(CAP * piece + t, n_row, stride=rows_out), :] = jnp.zeros((n_row, BS), jnp.float32)


def pack_kernel(n_row, n_col, slots_ref, cut_ref, ahead_ref, out_ref):
    piece = BS // n_row
    rows_out = CAP * piece + TABLE
    out_ref[...] = cut_ref[...]
    of_slot = lax.rem(iota((BS, BS), 1), CAP)
    field = iota((BS, BS), 0)
    mine = iota((n_col, BS), 0) == lax.div(iota((n_col, BS), 1), CAP)
    got = slots_ref[...].reshape(n_col, BS).astype(jnp.float32)

    def along(at):
        spread = jnp.where(field == at, 1.0, 0.0)
        return jnp.sum(jnp.where(mine, dot(got, spread), 0.0), axis=0, keepdims=True)

    used = lax.rem(iota((1, BS), 1), CAP).astype(jnp.float32) < along(2 * CAP)
    block_row = jnp.where(used, along(of_slot), -1.0)
    block_col = along(of_slot + CAP)
    out_ref[pl.ds(CAP * piece, n_row, stride=rows_out), :] = jnp.broadcast_to(block_row, (n_row, BS))
    out_ref[pl.ds(CAP * piece + 1, n_row, stride=rows_out), :] = jnp.broadcast_to(block_col, (n_row, BS))


def select_kernel(n_row, initial, *refs):
    got_ref, out_ref, plan_ref, most_ref = refs[-4:]
    piece = BS // n_row
    rows_in = CAP * piece + TABLE
    base = CAP * piece
    slots = CAP * n_row
    my_row, my_col, first = turned(lax.axis_index("row")), lax.axis_index("col"), 0 if initial else refs[0][0]

    def strided(start):
        return got_ref[pl.ds(start, n_row, stride=rows_in), :]

    block_row, block_col = strided(base), strided(base + 1)
    lane = iota((n_row, BS), 1)
    own_row, own_col = [], []
    for o in range(CAP):
        here = lane == my_col * CAP + o
        own_row.append(jnp.sum(jnp.where(here, block_row, 0.0), axis=1, keepdims=True))
        own_col.append(jnp.sum(jnp.where(here, block_col, 0.0), axis=1, keepdims=True))
    both = jnp.concatenate([block_row, block_col], axis=0)
    of_slot, of_k = iota((BS, 2 * BS), 0), iota((BS, 2 * BS), 1)
    k = iota((n_row, 2 * BS), 1)
    within = lax.rem(k, CB).astype(jnp.float32)
    place = (lax.div(k, CB) * CAP + 1).astype(jnp.float32)
    spread = [dot(both, jnp.where(of_slot == lax.div(of_k, CB) * CAP + e, 1.0, 0.0)) for e in range(CAP)]
    in_col = [spread[e][n_row:] == within for e in range(CAP)]
    tables = []
    for o in range(CAP):
        wanted = jnp.where(own_row[o] < 0.0, -2.0, own_row[o])
        found = jnp.zeros((n_row, 2 * BS), jnp.float32)
        for e in range(CAP):
            found = jnp.where(in_col[e] & (spread[e][:n_row] == wanted), place + e, found)
        tables.append(found)
    table = jnp.concatenate(tables, axis=0)
    holds_row = jnp.concatenate(own_row, axis=0).astype(jnp.int32)
    holds_col = jnp.concatenate(own_col, axis=0).astype(jnp.int32)
    inner = turned(lax.rem(iota((slots, 1), 0), n_row)) * RB + holds_row
    valid = holds_row >= 0
    wide = iota((slots, BS), 1)
    at_head = jnp.where((wide == inner) & valid, 1.0, 0.0)
    at_tail = jnp.where((wide + BS == inner) & valid, 1.0, 0.0)
    of_col = jnp.where(wide == holds_col, 1.0, 0.0)
    nt = ((1,), (1,))
    m = (dot(table[:, :BS], at_head, nt) + dot(table[:, BS:], at_tail, nt)) * dot(of_col, of_col, nt)
    need = m[:n_row]
    for o in range(1, CAP):
        need = jnp.maximum(need, m[o * n_row : (o + 1) * n_row])
    need = jnp.where(need > 0.5, 1.0, 0.0)
    before = jnp.where(iota((slots, slots), 0) < iota((slots, slots), 1), 1.0, 0.0)
    rank = dot(need, before).astype(jnp.int32) - first
    rank = jnp.where(need > 0.5, rank, -1)
    chosen = jnp.concatenate([jnp.where(rank == p, 1.0, 0.0) for p in range(ROUND)], axis=0)
    rows = jnp.concatenate(
        [jnp.concatenate([strided(e * piece + q) for e in range(CAP)], axis=0) for q in range(piece)], axis=1
    )
    pick = jnp.concatenate([chosen.astype(jnp.bfloat16)] * 2, axis=1)
    part = dot(pick, jnp.concatenate(split(rows, 2), axis=0))
    for q in range(piece):
        for p in range(ROUND):
            out_ref[pl.ds(p * piece + q, n_row, stride=ROUND * piece), :] = part[
                p * n_row : (p + 1) * n_row, q * BS : (q + 1) * BS
            ]
    mine = iota((n_row, BS), 0) == my_row

    def own(a, n):
        return [jnp.sum(jnp.where(mine, a[i * n_row : (i + 1) * n_row], 0.0), axis=0, keepdims=True) for i in range(n)]

    own_m = jnp.concatenate(own(m, CAP) + [jnp.zeros((4, BS), jnp.float32)], axis=0)
    own_chosen = jnp.concatenate(own(chosen, ROUND) + [jnp.zeros((BS - ROUND, BS), jnp.float32)], axis=0)
    needed = jnp.sum(need, axis=1, keepdims=True)
    most_ref[0, 0] = (jnp.max(needed) + 0.5).astype(jnp.int32)
    here = jnp.sum(jnp.sum(own_chosen, axis=1, keepdims=True), axis=0, keepdims=True)
    plan = jnp.where(iota((8, BS), 0) == 7, here, dot(own_m, own_chosen, nt))
    plan_ref[...] = (plan + 0.5).astype(jnp.int32)


def each_product(plan_ref, act):
    def tile(p, n):
        for o in range(CAP):
            used = plan_ref[o, p] > 0

            @pl.when(used)
            def _():
                act(n, o, p)

            n = n + used.astype(jnp.int32)
        return n

    lax.fori_loop(0, plan_ref[7, 0], tile, 0)


def fetch_kernel(plan_ref, x_ref, out_ref, sems):
    def copy(n, o, p):
        return pltpu.make_async_copy(x_ref.at[plan_ref[o, p] - 1], out_ref.at[n], sems.at[n])

    def start(n, o, p):
        @pl.when(n < AHEAD)
        def _():
            copy(n, o, p).start()

    def wait(n, o, p):
        @pl.when(n < AHEAD)
        def _():
            copy(n, o, p).wait()

    each_product(plan_ref, start)
    each_product(plan_ref, wait)


def multiply_kernel(n_row, plan_ref, base_ref, got_ref, ahead_ref, x_ref, out_ref, x_buf, sem):
    piece = BS // n_row
    out_ref[...] = base_ref[...]

    def tile(p, n):
        s_tile = jnp.concatenate(
            [got_ref[pl.ds(p * piece + q, n_row, stride=ROUND * piece), :] for q in range(piece)], axis=0
        )
        s_high, s_low = split(s_tile, 2)

        def subtract(o, x):
            x_high, x_low = split(x, 2)
            product = dot(x_high, s_high) + (dot(x_high, s_low) + dot(x_low, s_high))
            out_ref[o] = out_ref[o] - 0.5 * product

        for o in range(CAP):
            used = plan_ref[o, p] > 0

            @pl.when(used & (n < AHEAD))
            def _(n=n):
                subtract(o, ahead_ref[jnp.minimum(n, AHEAD - 1)])

            @pl.when(used & (n >= AHEAD))
            def _():
                copy = pltpu.make_async_copy(x_ref.at[plan_ref[o, p] - 1], x_buf, sem)
                copy.start()
                copy.wait()
                subtract(o, x_buf[...])

            n = n + used.astype(jnp.int32)
        return n

    lax.fori_loop(0, plan_ref[7, 0], tile, 0)


def per_device(n_row, n_col, x_stack, s_stack, entries, counts):
    smem = pl.BlockSpec(memory_space=pltpu.SMEM)
    vmem = pl.BlockSpec(memory_space=pltpu.VMEM)
    hbm = pl.BlockSpec(memory_space=pltpu.HBM)
    params = pltpu.CompilerParams(vmem_limit_bytes=VMEM_LIMIT)
    piece = BS // n_row
    rows_out = CAP * piece + TABLE
    x_own = x_stack[0, 0]
    row_panel = lax.all_gather(x_stack[0], "col", axis=0, tiled=True).reshape(n_col * CAP, BS, BS)

    valid = jnp.arange(CAP, dtype=jnp.int32) < counts[0, 0]
    base = jnp.where(valid[:, None, None], 1.5 * x_own, 0.0)
    own = jnp.concatenate([entries.reshape(2 * CAP), counts.reshape(1), jnp.zeros((BS - 2 * CAP - 1,), jnp.int32)])
    slots = lax.all_to_all(jnp.broadcast_to(own[None, None], (n_col, 1, BS)), "col", 0, 0)
    cut = pl.pallas_call(
        functools.partial(cut_kernel, n_row),
        out_shape=jax.ShapeDtypeStruct((n_row * rows_out, BS), jnp.float32),
        in_specs=[vmem],
        out_specs=vmem,
        compiler_params=params,
        cost_estimate=pl.CostEstimate(flops=0, bytes_accessed=2**22, transcendentals=0),
        name="cut",
    )(s_stack[0, 0])
    packed = pl.pallas_call(
        functools.partial(pack_kernel, n_row, n_col),
        out_shape=jax.ShapeDtypeStruct((n_row * rows_out, BS), jnp.float32),
        in_specs=[vmem, vmem, pl.BlockSpec(memory_space=pl.ANY)],
        out_specs=vmem,
        compiler_params=params,
        name="pack",
    )(slots, cut, base)
    parts = rows_out // 2
    pieces = lax.all_to_all(packed.reshape(n_row, parts, 2, BS), "row", 0, 0, axis_index_groups=[[int(format(i, "05b")[::-1], 2) for i in range(n_row)]]).reshape(n_row * rows_out, BS)

    def select(*first):
        chosen, plan, most = pl.pallas_call(
            functools.partial(select_kernel, n_row, not first),
            out_shape=(
                jax.ShapeDtypeStruct((n_row * ROUND * piece, BS), jnp.float32),
                jax.ShapeDtypeStruct((8, BS), jnp.int32),
                jax.ShapeDtypeStruct((1, 1), jnp.int32),
            ),
            in_specs=[smem] * len(first) + [vmem],
            out_specs=(vmem, vmem, smem),
            compiler_params=params,
            name="select",
        )(*first, pieces)
        tiles = lax.all_to_all(chosen.reshape(n_row, ROUND * piece, BS), "row", 0, 0, axis_index_groups=[[int(format(i, "05b")[::-1], 2) for i in range(n_row)]])
        return tiles.reshape(n_row * ROUND * piece, BS), plan, most[0, 0]

    def fetch(plan):
        return pl.pallas_call(
            fetch_kernel,
            out_shape=jax.ShapeDtypeStruct((AHEAD, BS, BS), jnp.float32),
            in_specs=[smem, hbm],
            out_specs=vmem,
            scratch_shapes=[pltpu.SemaphoreType.DMA((AHEAD,))],
            compiler_params=params,
            cost_estimate=pl.CostEstimate(flops=0, bytes_accessed=2**23, transcendentals=0),
            name="fetch",
        )(plan, row_panel)

    def multiply(tiles, plan, base, x_tiles):
        return pl.pallas_call(
            functools.partial(multiply_kernel, n_row),
            out_shape=jax.ShapeDtypeStruct((CAP, BS, BS), jnp.float32),
            in_specs=[smem, vmem, vmem, vmem, hbm],
            out_specs=vmem,
            scratch_shapes=[pltpu.VMEM((BS, BS), jnp.float32), pltpu.SemaphoreType.DMA],
            compiler_params=params,
            name="multiply",
        )(plan, base, tiles, x_tiles, row_panel)

    tiles, plan, most = select()

    def another(state):
        first, partial = state
        more, where, _ = select(first.reshape(1))
        return first + ROUND, multiply(more, where, partial, fetch(where))

    x_tiles = fetch(plan)
    result = lax.cond(
        most > ROUND,
        lambda ahead: lax.while_loop(
            lambda state: state[0] < most, another, (jnp.int32(ROUND), multiply(tiles, plan, base, ahead))
        )[1],
        lambda ahead: multiply(tiles, plan, base, ahead),
        x_tiles,
    )
    return result[None, None]


def solution(mesh):
    return jax.shard_map(
        functools.partial(per_device, mesh.shape["row"], mesh.shape["col"]),
        mesh=mesh,
        in_specs=(
            P("row", "col", None, None, None),
            P("row", "col", None, None, None),
            P("row", "col", None, None),
            P("row", "col"),
        ),
        out_specs=P("row", "col", None, None, None),
        check_vma=False,
    )
```

```python
import functools

import jax
import jax.numpy as jnp
from jax import lax
from jax.experimental import pallas as pl
from jax.experimental.pallas import tpu as pltpu
from jax.sharding import PartitionSpec as P

RB = 6
CB = 8
CAP = 4
BS = 128
ROUND = 12
AHEAD = 16
TABLE = 2

VMEM_LIMIT = 24 * 1024 * 1024


def iota(shape, dim):
    return lax.broadcasted_iota(jnp.int32, shape, dim)


def turned(i):
    out = 0
    for bit in range(5):
        out = out + lax.rem(lax.div(i, 2**bit), 2) * 2 ** (4 - bit)
    return out


def dot(a, b, dims=((1,), (0,))):
    return lax.dot_general(a, b, (dims, ((), ())), preferred_element_type=jnp.float32)


def split(a, parts):
    out = []
    for _ in range(parts):
        out.append(a.astype(jnp.bfloat16))
        a = a - out[-1].astype(jnp.float32)
    return out


def cut_kernel(n_row, s_ref, out_ref):
    piece = BS // n_row
    rows_out = CAP * piece + TABLE
    for e in range(CAP):
        for q in range(piece):
            for i in range(n_row):
                at = int(format(i, "05b")[::-1], 2) * rows_out + e * piece + q
                out_ref[at : at + 1, :] = s_ref[e, q * n_row + i : q * n_row + i + 1, :]
    for t in range(TABLE):
        out_ref[pl.ds(CAP * piece + t, n_row, stride=rows_out), :] = jnp.zeros((n_row, BS), jnp.float32)


def pack_kernel(n_row, n_col, slots_ref, cut_ref, ahead_ref, out_ref):
    piece = BS // n_row
    rows_out = CAP * piece + TABLE
    out_ref[...] = cut_ref[...]
    of_slot = lax.rem(iota((BS, BS), 1), CAP)
    field = iota((BS, BS), 0)
    mine = iota((n_col, BS), 0) == lax.div(iota((n_col, BS), 1), CAP)
    got = slots_ref[...].reshape(n_col, BS).astype(jnp.float32)

    def along(at):
        spread = jnp.where(field == at, 1.0, 0.0)
        return jnp.sum(jnp.where(mine, dot(got, spread), 0.0), axis=0, keepdims=True)

    used = lax.rem(iota((1, BS), 1), CAP).astype(jnp.float32) < along(2 * CAP)
    block_row = jnp.where(used, along(of_slot), -1.0)
    block_col = along(of_slot + CAP)
    out_ref[pl.ds(CAP * piece, n_row, stride=rows_out), :] = jnp.broadcast_to(block_row, (n_row, BS))
    out_ref[pl.ds(CAP * piece + 1, n_row, stride=rows_out), :] = jnp.broadcast_to(block_col, (n_row, BS))


def select_kernel(n_row, initial, *refs):
    got_ref, out_ref, plan_ref, most_ref = refs[-4:]
    piece = BS // n_row
    rows_in = CAP * piece + TABLE
    base = CAP * piece
    slots = CAP * n_row
    my_row, my_col, first = lax.axis_index("row"), lax.axis_index("col"), 0 if initial else refs[0][0]

    def strided(start):
        return got_ref[pl.ds(start, n_row, stride=rows_in), :]

    block_row, block_col = strided(base), strided(base + 1)
    lane = iota((n_row, BS), 1)
    own_row, own_col = [], []
    for o in range(CAP):
        here = lane == my_col * CAP + o
        own_row.append(jnp.sum(jnp.where(here, block_row, 0.0), axis=1, keepdims=True))
        own_col.append(jnp.sum(jnp.where(here, block_col, 0.0), axis=1, keepdims=True))
    both = jnp.concatenate([block_row, block_col], axis=0)
    of_slot, of_k = iota((BS, 2 * BS), 0), iota((BS, 2 * BS), 1)
    k = iota((n_row, 2 * BS), 1)
    within = lax.rem(k, CB).astype(jnp.float32)
    place = (lax.div(k, CB) * CAP + 1).astype(jnp.float32)
    spread = [dot(both, jnp.where(of_slot == lax.div(of_k, CB) * CAP + e, 1.0, 0.0)) for e in range(CAP)]
    in_col = [spread[e][n_row:] == within for e in range(CAP)]
    tables = []
    for o in range(CAP):
        wanted = jnp.where(own_row[o] < 0.0, -2.0, own_row[o])
        found = jnp.zeros((n_row, 2 * BS), jnp.float32)
        for e in range(CAP):
            found = jnp.where(in_col[e] & (spread[e][:n_row] == wanted), place + e, found)
        tables.append(found)
    table = jnp.concatenate(tables, axis=0)
    holds_row = jnp.concatenate(own_row, axis=0).astype(jnp.int32)
    holds_col = jnp.concatenate(own_col, axis=0).astype(jnp.int32)
    inner = lax.rem(iota((slots, 1), 0), n_row) * RB + holds_row
    valid = holds_row >= 0
    wide = iota((slots, BS), 1)
    at_head = jnp.where((wide == inner) & valid, 1.0, 0.0)
    at_tail = jnp.where((wide + BS == inner) & valid, 1.0, 0.0)
    of_col = jnp.where(wide == holds_col, 1.0, 0.0)
    nt = ((1,), (1,))
    m = (dot(table[:, :BS], at_head, nt) + dot(table[:, BS:], at_tail, nt)) * dot(of_col, of_col, nt)
    need = m[:n_row]
    for o in range(1, CAP):
        need = jnp.maximum(need, m[o * n_row : (o + 1) * n_row])
    need = jnp.where(need > 0.5, 1.0, 0.0)
    before = jnp.where(iota((slots, slots), 0) < iota((slots, slots), 1), 1.0, 0.0)
    rank = dot(need, before).astype(jnp.int32) - first
    rank = jnp.where(need > 0.5, rank, -1)
    order = jnp.where(iota((n_row, n_row), 1) == turned(iota((n_row, n_row), 0)), 1.0, 0.0)
    rank = dot(order, rank.astype(jnp.float32)).astype(jnp.int32)
    chosen = jnp.concatenate([jnp.where(rank == p, 1.0, 0.0) for p in range(ROUND)], axis=0)
    rows = jnp.concatenate(
        [jnp.concatenate([strided(e * piece + q) for e in range(CAP)], axis=0) for q in range(piece)], axis=1
    )
    pick = jnp.concatenate([chosen.astype(jnp.bfloat16)] * 2, axis=1)
    part = dot(pick, jnp.concatenate(split(rows, 2), axis=0))
    for q in range(piece):
        for p in range(ROUND):
            out_ref[pl.ds(p * piece + q, n_row, stride=ROUND * piece), :] = part[
                p * n_row : (p + 1) * n_row, q * BS : (q + 1) * BS
            ]

    def own(a, n, at):
        return [jnp.sum(jnp.where(iota((n_row, BS), 0) == at, a[i * n_row : (i + 1) * n_row], 0.0), axis=0, keepdims=True) for i in range(n)]

    own_m = jnp.concatenate(own(m, CAP, my_row) + [jnp.zeros((4, BS), jnp.float32)], axis=0)
    own_chosen = jnp.concatenate(own(chosen, ROUND, turned(my_row)) + [jnp.zeros((BS - ROUND, BS), jnp.float32)], axis=0)
    needed = jnp.sum(need, axis=1, keepdims=True)
    most_ref[0, 0] = (jnp.max(needed) + 0.5).astype(jnp.int32)
    here = jnp.sum(jnp.sum(own_chosen, axis=1, keepdims=True), axis=0, keepdims=True)
    plan = jnp.where(iota((8, BS), 0) == 7, here, dot(own_m, own_chosen, nt))
    plan_ref[...] = (plan + 0.5).astype(jnp.int32)


def each_product(plan_ref, act):
    def tile(p, n):
        for o in range(CAP):
            used = plan_ref[o, p] > 0

            @pl.when(used)
            def _():
                act(n, o, p)

            n = n + used.astype(jnp.int32)
        return n

    return lax.fori_loop(0, plan_ref[7, 0], tile, 0)


def fetch_kernel(plan_ref, x_ref, out_ref, sems):
    def copy(n, o, p):
        return pltpu.make_async_copy(x_ref.at[plan_ref[o, p] - 1], out_ref.at[n], sems.at[n])

    def start(n, o, p):
        @pl.when(n < AHEAD)
        def _():
            copy(n, o, p).start()

    started = each_product(plan_ref, start)

    @pl.loop(0, jnp.minimum(started, AHEAD))
    def _(n):
        pltpu.make_async_copy(x_ref.at[0], out_ref.at[n], sems.at[n]).wait()


def multiply_kernel(n_row, plan_ref, base_ref, got_ref, ahead_ref, x_ref, out_ref, x_buf, sem):
    piece = BS // n_row
    out_ref[...] = base_ref[...]

    def tile(p, n):
        s_tile = jnp.concatenate(
            [got_ref[pl.ds(p * piece + q, n_row, stride=ROUND * piece), :] for q in range(piece)], axis=0
        )
        s_high, s_low = split(s_tile, 2)

        def subtract(o, x):
            x_high, x_low = split(x, 2)
            product = dot(x_high, s_high) + (dot(x_high, s_low) + dot(x_low, s_high))
            out_ref[o] = out_ref[o] - 0.5 * product

        for o in range(CAP):
            used = plan_ref[o, p] > 0

            @pl.when(used & (n < AHEAD))
            def _(n=n):
                subtract(o, ahead_ref[jnp.minimum(n, AHEAD - 1)])

            @pl.when(used & (n >= AHEAD))
            def _():
                copy = pltpu.make_async_copy(x_ref.at[plan_ref[o, p] - 1], x_buf, sem)
                copy.start()
                copy.wait()
                subtract(o, x_buf[...])

            n = n + used.astype(jnp.int32)
        return n

    lax.fori_loop(0, plan_ref[7, 0], tile, 0)


def per_device(n_row, n_col, x_stack, s_stack, entries, counts):
    smem = pl.BlockSpec(memory_space=pltpu.SMEM)
    vmem = pl.BlockSpec(memory_space=pltpu.VMEM)
    hbm = pl.BlockSpec(memory_space=pltpu.HBM)
    params = pltpu.CompilerParams(vmem_limit_bytes=VMEM_LIMIT)
    piece = BS // n_row
    rows_out = CAP * piece + TABLE
    x_own = x_stack[0, 0]
    row_panel = lax.all_gather(x_stack[0], "col", axis=0, tiled=True).reshape(n_col * CAP, BS, BS)

    valid = jnp.arange(CAP, dtype=jnp.int32) < counts[0, 0]
    base = jnp.where(valid[:, None, None], 1.5 * x_own, 0.0)
    own = jnp.concatenate([entries.reshape(2 * CAP), counts.reshape(1), jnp.zeros((BS - 2 * CAP - 1,), jnp.int32)])
    slots = lax.all_to_all(jnp.broadcast_to(own[None, None], (n_col, 1, BS)), "col", 0, 0)
    cut = pl.pallas_call(
        functools.partial(cut_kernel, n_row),
        out_shape=jax.ShapeDtypeStruct((n_row * rows_out, BS), jnp.float32),
        in_specs=[vmem],
        out_specs=vmem,
        compiler_params=params,
        cost_estimate=pl.CostEstimate(flops=0, bytes_accessed=2**22, transcendentals=0),
        name="cut",
    )(s_stack[0, 0])
    packed = pl.pallas_call(
        functools.partial(pack_kernel, n_row, n_col),
        out_shape=jax.ShapeDtypeStruct((n_row * rows_out, BS), jnp.float32),
        in_specs=[vmem, vmem, pl.BlockSpec(memory_space=pl.ANY)],
        out_specs=vmem,
        compiler_params=params,
        name="pack",
    )(slots, cut, base)
    parts = rows_out // 2
    pieces = lax.all_to_all(packed.reshape(n_row, parts, 2, BS), "row", 0, 0).reshape(n_row * rows_out, BS)

    def select(*first):
        chosen, plan, most = pl.pallas_call(
            functools.partial(select_kernel, n_row, not first),
            out_shape=(
                jax.ShapeDtypeStruct((n_row * ROUND * piece, BS), jnp.float32),
                jax.ShapeDtypeStruct((8, BS), jnp.int32),
                jax.ShapeDtypeStruct((1, 1), jnp.int32),
            ),
            in_specs=[smem] * len(first) + [vmem],
            out_specs=(vmem, vmem, smem),
            compiler_params=params,
            name="select",
        )(*first, pieces)
        tiles = lax.all_to_all(chosen.reshape(n_row, ROUND * piece, BS), "row", 0, 0, axis_index_groups=[[int(format(i, "05b")[::-1], 2) for i in range(n_row)]])
        return tiles.reshape(n_row * ROUND * piece, BS), plan, most[0, 0]

    def fetch(plan):
        return pl.pallas_call(
            fetch_kernel,
            out_shape=jax.ShapeDtypeStruct((AHEAD, BS, BS), jnp.float32),
            in_specs=[smem, hbm],
            out_specs=vmem,
            scratch_shapes=[pltpu.SemaphoreType.DMA((AHEAD,))],
            compiler_params=params,
            cost_estimate=pl.CostEstimate(flops=0, bytes_accessed=2**23, transcendentals=0),
            name="fetch",
        )(plan, row_panel)

    def multiply(tiles, plan, base, x_tiles):
        return pl.pallas_call(
            functools.partial(multiply_kernel, n_row),
            out_shape=jax.ShapeDtypeStruct((CAP, BS, BS), jnp.float32),
            in_specs=[smem, vmem, vmem, vmem, hbm],
            out_specs=vmem,
            scratch_shapes=[pltpu.VMEM((BS, BS), jnp.float32), pltpu.SemaphoreType.DMA],
            compiler_params=params,
            name="multiply",
        )(plan, base, tiles, x_tiles, row_panel)

    tiles, plan, most = select()

    def another(state):
        first, partial = state
        more, where, _ = select(first.reshape(1))
        return first + ROUND, multiply(more, where, partial, fetch(where))

    x_tiles = fetch(plan)
    result = lax.cond(
        most > ROUND,
        lambda ahead: lax.while_loop(
            lambda state: state[0] < most, another, (jnp.int32(ROUND), multiply(tiles, plan, base, ahead))
        )[1],
        lambda ahead: multiply(tiles, plan, base, ahead),
        x_tiles,
    )
    return result[None, None]


def solution(mesh):
    return jax.shard_map(
        functools.partial(per_device, mesh.shape["row"], mesh.shape["col"]),
        mesh=mesh,
        in_specs=(
            P("row", "col", None, None, None),
            P("row", "col", None, None, None),
            P("row", "col", None, None),
            P("row", "col"),
        ),
        out_specs=P("row", "col", None, None, None),
        check_vma=False,
    )
```
